32 devices in a mesh: expert: 16 (over z, y, core), group: 2 (over x).
Axes of the slice: x: 2, y: 2, z: 4, core: 2. Of those that a mesh axis runs over, the one named last changes fastest.
Arguments:
- tokens: bfloat16 [2, 2048, 2048], P('group', 'expert'), may hold values from -6 to 6
- routes: int32 [2, 2048, 8], P('group', 'expert'), may hold values from 0 to 15, all different within a row; in each aligned block of 128 rows (0 to 127, 128 to 255, ..., all dimensions but the last counted through in order) at most 96 rows name the same one
- gate_up: bfloat16 [16, 2048, 1536], P('expert'), may hold values from -0.125 to 0.125
- down_weight: bfloat16 [16, 2048, 768], P('expert'), may hold values from -0.21875 to 0.21875
- sketch: bfloat16 [16, 2048, 256], P('expert'), may hold values from -6 to 6
Outputs:
- gram: float32 [16, 768, 768], P('expert', 'group')
- power: float32 [16, 2048, 256], P('expert', 'group')
The draws below stay inside these ranges and needn't reach their ends.
Inputs may be any that keep to these rules, and one draw needn't show every extreme that they name: `routes`: each token names 8 different experts; among the rows of one device no expert is named by more than 96 tokens, and in every draw some expert is named by exactly 96 tokens of some device.
All inputs are finite; a program needn't handle non-finite values.
Results may differ from the reference program's by a relative error of at most 0.0042.
Values may be sent and summed in bfloat16 or wider, within the bound.
No kernel may reach another device: no remote copies, remote signals or barrier semaphores. Data moves between devices by JAX's collectives and lax.ppermute only.
A program may use at most 64 MiB of HBM per device.

```python
import math
import jax
import jax.numpy as jnp
import numpy as np
from jax import lax

D = 2048
FF = 768
RANK = 256
TOPK = 8
TOK_DEV = 128
EXPERTS = 16
GTOK = 2048
CAP = 96
MAXROWS = 3072
N_GROUP = 2


def block_scale(key, dims, pieces, smallest, top_value):
    gain = 1.0
    for axis_at, blocks in pieces:
        steps = jax.random.uniform(jax.random.fold_in(jax.random.fold_in(key, 6), axis_at), (blocks,), jnp.float32, smallest / len(pieces), top_value / len(pieces))
        gain = gain * jnp.repeat(jnp.exp(steps), dims[axis_at] // blocks).reshape((-1,) + (1,) * (len(dims) - 1 - axis_at))
    return gain


def shared_out(own_key, own, number, rows, amount, top, reach, lean):
    sequence = jax.random.permutation(own_key, amount)
    crowded, ordinary = portions_of(amount, rows * top, reach, lean, True), portions_of(amount, rows * top, reach, lean, False)
    places = jnp.arange(amount)

    def named(sizes, offset_by):
        used = int((sizes > 0).sum())
        fixed = max(1, used // 4)
        passed = fixed + (places - fixed + offset_by * (used - fixed)) % max(1, amount - fixed)
        return jnp.zeros((amount,), jnp.int32).at[sequence[jnp.where(places < fixed, places, passed)]].set(jnp.asarray(sizes, jnp.int32))

    sizes = jnp.where(number % 4 == 0, named(crowded, number // 4), named(ordinary, number - number // 4 - 1))
    mixed = jax.random.permutation(jax.random.fold_in(own, 3), amount)
    giver, sink = mixed[0:amount // 2 * 2:2], mixed[1:amount // 2 * 2:2]
    slack = jnp.minimum(sizes[giver] - 1, reach - sizes[sink]) // 2
    slack = jnp.where((giver == sequence[0]) | (sink == sequence[0]) | (sizes[sink] == 0), 0, jnp.maximum(slack, 0))
    passed = jax.random.randint(jax.random.fold_in(own, 4), (amount // 2,), 0, 1 << 20) % (slack + 1)
    sizes = sizes.at[giver].add(-passed).at[sink].add(passed)
    labels = jnp.searchsorted(jnp.cumsum(sizes), jnp.arange(rows * top), side="right").astype(jnp.int32)
    table = labels.reshape(top, rows).T
    table = table[jax.random.permutation(jax.random.fold_in(own, 1), rows)]
    offset_by = jax.random.randint(jax.random.fold_in(own, 2), (rows, 1), 0, top)
    return jnp.take_along_axis(table, (jnp.arange(top)[None, :] + offset_by) % top, axis=1)


def portions_of(number_of, total, bound, skew, full):
    loads = [(1 << 20) // math.isqrt(grade ** skew) + 1 for grade in range(1, number_of + 1)]
    largest = bound if full else min(bound, max(-(-total // number_of), total * loads[0] // sum(loads)))
    least = 1 if total - largest >= number_of - 1 else 0
    holding, spare = [largest] + [least] * (number_of - 1), total - largest - least * (number_of - 1)
    while spare > 0:
        candidates = [i for i in range(1, number_of) if holding[i] < largest] or [i for i in range(1, number_of) if holding[i] < bound]
        whole, budget = sum([loads[i] for i in candidates]), spare
        for i in candidates:
            addition = min(bound - holding[i], max(1, budget * loads[i] // whole), spare)
            holding[i] = holding[i] + addition
            spare = spare - addition
    return np.array(holding)


def centred(stream_key, dims, spread, limit, shards=(), held_as=jnp.bfloat16):
    array = jax.random.normal(stream_key, dims, jnp.float32) * spread
    if len(shards) > 0:
        array = block_scale(stream_key, dims, shards, -0.22, 0.18) * array
    return jnp.clip(array, min=-limit, max=limit).astype(held_as)


def setup_inputs(seed: int = 0) -> dict:
    key_of = jax.random.split(jax.random.key(seed), 6)
    tokens = centred(key_of[0], (N_GROUP, GTOK, D), 1.0, 6.0, ((0, 2), (1, 16)))
    routes_keys = jax.random.split(jax.random.fold_in(key_of[1], 1), N_GROUP * GTOK // TOK_DEV)
    routes_turns = jax.random.permutation(jax.random.fold_in(key_of[1], 3), N_GROUP * GTOK // TOK_DEV)
    routes = jax.vmap(lambda own, number: shared_out(jax.random.fold_in(key_of[1], 2), own, number, TOK_DEV, EXPERTS, TOPK, CAP, 2))(routes_keys, routes_turns).reshape((N_GROUP, GTOK, TOPK))
    gate_up = centred(key_of[2], (EXPERTS, D, 2 * FF), D ** -0.5, 0.125, ((0, 16),))
    down_weight = centred(key_of[3], (EXPERTS, D, FF), FF ** -0.5, 0.21875, ((0, 16),))
    sketch = centred(key_of[4], (EXPERTS, D, RANK), 1.0, 6.0, ((0, 16),))
    return {"tokens": tokens, "routes": routes, "gate_up": gate_up, "down_weight": down_weight, "sketch": sketch}


def reference(tokens, routes, gate_up, down_weight, sketch):
    all_rows = N_GROUP * GTOK
    flat_tokens = tokens.reshape(all_rows, D)
    flat_routes = routes.reshape(all_rows, TOPK)
    scale_factor = 1.0 / (TOK_DEV * TOPK * N_GROUP)
    positions = jnp.arange(all_rows, dtype=jnp.int32)

    def expert_step(inputs):
        expert_id, expert_weight, w_down, sketch_e = inputs
        chosen = jnp.any(flat_routes == expert_id, axis=1)
        order_key = jnp.where(chosen, positions, positions + all_rows)
        picked = jnp.argsort(order_key)[:MAXROWS].astype(jnp.int32)
        gathered = flat_tokens[picked] * chosen[picked].astype(jnp.bfloat16)[:, None]
        projected = jnp.dot(gathered, expert_weight, preferred_element_type=jnp.float32)
        hidden = (jax.nn.silu(projected[:, :FF]) * projected[:, FF:]).astype(jnp.bfloat16)
        gram_matrix = lax.dot_general(hidden, hidden, (((0,), (0,)), ((), ())), preferred_element_type=jnp.float32) * scale_factor
        probe_cols = sketch_e
        image_full = None
        for sweep_pass in range(2):
            reduced = lax.dot_general(w_down, probe_cols, (((0,), (0,)), ((), ())), preferred_element_type=jnp.float32)
            panel_bf = jnp.dot(gram_matrix, reduced, precision=lax.Precision.HIGHEST).astype(jnp.bfloat16)
            image_full = jnp.dot(w_down, panel_bf, preferred_element_type=jnp.float32)
            if sweep_pass == 0:
                probe_cols = (image_full * lax.rsqrt(lax.optimization_barrier(jnp.mean(image_full * image_full, axis=0, keepdims=True)) + 1e-06)).astype(jnp.bfloat16)
        return (gram_matrix, image_full)
    expert_ids = jnp.arange(EXPERTS, dtype=jnp.int32)
    gram, power = lax.map(expert_step, (expert_ids, gate_up, down_weight, sketch))
    return (gram, power)
```

```python
import functools

import jax
import jax.numpy as jnp
from jax import lax
from jax.experimental import pallas as pl
from jax.experimental.pallas import tpu as pltpu
from jax.sharding import PartitionSpec as P

TOPK = 8
LANES = 128
ID_ROWS = 16
BLOCKS_PER_CALL = 4
NT = (((1,), (1,)), ((), ()))
BF16 = jnp.bfloat16
F32 = jnp.float32
VMEM = pl.BlockSpec(memory_space=pltpu.VMEM)
SMEM = pl.BlockSpec(memory_space=pltpu.SMEM)
MIB = 1 << 20


def params(mib):
    return pltpu.CompilerParams(vmem_limit_bytes=mib * MIB)


def half_rows(tok_dev, width):
    return tok_dev // 2 * (width // LANES) + ID_ROWS


def pack_kernel(tokens_ref, routes_ref, out_ref):
    tok_dev, width = tokens_ref.shape
    top = routes_ref.shape[1]
    half, tiles = tok_dev // 2, width // LANES
    rows = half_rows(tok_dev, width)
    eye = (
        lax.broadcasted_iota(jnp.int32, (ID_ROWS, top), 0)
        == lax.broadcasted_iota(jnp.int32, (ID_ROWS, top), 1)
    ).astype(BF16)
    ids = lax.dot_general(
        eye, routes_ref[...].astype(F32).astype(BF16), NT, preferred_element_type=F32
    )
    lane = lax.broadcasted_iota(jnp.int32, ids.shape, 1)
    row = lax.broadcasted_iota(jnp.int32, ids.shape, 0)
    for h in range(2):
        for i in range(half // 16):
            for k in range(tiles):
                at = h * rows + (i * tiles + k) * 16
                out_ref[at : at + 16, :] = tokens_ref[
                    h * half + i * 16 : h * half + (i + 1) * 16, k * LANES : (k + 1) * LANES
                ]
        mine = (lane >= h * half) & (lane < (h + 1) * half) & (row < top)
        out_ref[(h + 1) * rows - ID_ROWS : (h + 1) * rows, :tok_dev] = jnp.where(
            mine, ids, -1.0
        ).astype(BF16)


def pack(tokens, routes):
    tok_dev, width = tokens.shape
    return pl.pallas_call(
        pack_kernel,
        out_shape=jax.ShapeDtypeStruct((2 * half_rows(tok_dev, width), LANES), BF16),
        in_specs=[VMEM, VMEM],
        out_specs=VMEM,
        compiler_params=params(8),
        cost_estimate=pl.CostEstimate(flops=0, bytes_accessed=tokens.size * 4, transcendentals=0),
    )(tokens, routes)


def transpose_kernel(in_ref, out_ref):
    def step(j, _):
        at = pl.multiple_of(j * LANES, LANES)
        out_ref[pl.ds(at, LANES), :] = in_ref[:, pl.ds(at, LANES)].T
        return 0

    lax.fori_loop(0, in_ref.shape[1] // LANES, step, 0)


def transposed(array):
    return pl.pallas_call(
        transpose_kernel,
        out_shape=jax.ShapeDtypeStruct(array.shape[::-1], array.dtype),
        in_specs=[VMEM],
        out_specs=VMEM,
        compiler_params=params(8),
        cost_estimate=pl.CostEstimate(flops=0, bytes_accessed=array.size * 8, transcendentals=0),
    )(array)


def reduce_kernel(w_ref, sketch_ref, wt_ref, out_ref):
    transpose_kernel(w_ref, wt_ref)
    out_ref[...] = jnp.dot(wt_ref[...], sketch_ref[...], preferred_element_type=F32)


def reduced_first(w_down, sketch):
    hidden_width, width = w_down.shape[1], w_down.shape[0]
    return pl.pallas_call(
        reduce_kernel,
        out_shape=(
            jax.ShapeDtypeStruct((hidden_width, width), BF16),
            jax.ShapeDtypeStruct((hidden_width, sketch.shape[1]), F32),
        ),
        in_specs=[VMEM, VMEM],
        out_specs=(VMEM, VMEM),
        compiler_params=params(8),
        cost_estimate=pl.CostEstimate(
            flops=2 * w_down.size * sketch.shape[1], bytes_accessed=w_down.size * 8, transcendentals=0
        ),
    )(w_down, sketch)


def upper_tiles(count):
    return [(a, b) for a in range(count) for b in range(a, count)]


def gram_step(hidden_width):
    return 2 * LANES if hidden_width % (2 * LANES) == 0 else LANES


def ffn_kernel(*refs, tok_dev, width, sources, has_gram, scale):
    operands = 1 + max(max(first[0], second[0]) for first, second in sources)
    expert_ref, weight_ref = refs[0], refs[1]
    pieces = refs[2 : 2 + operands]
    rest = list(refs[2 + operands :])
    gram_in = rest.pop(0) if has_gram else None
    gram_out = rest.pop(0)
    packed_out = rest.pop(0) if scale is not None else None
    x_ref, mask_ref, hidden_ref = rest
    half, tiles = tok_dev // 2, width // LANES
    expert = expert_ref[0].astype(F32)
    for b, block in enumerate(sources):
        hits = None
        for h, (operand, first) in enumerate(block):
            piece = pieces[operand]
            for i in range(half // 16):
                for k in range(tiles):
                    at = first + (i * tiles + k) * 16
                    row = b * tok_dev + h * half + i * 16
                    x_ref[row : row + 16, k * LANES : (k + 1) * LANES] = piece[at : at + 16, :]
            at = first + half * tiles
            found = (piece[at : at + ID_ROWS, :tok_dev].astype(F32) == expert).astype(F32)
            hits = found if hits is None else hits + found
        mask_ref[0:1, b * tok_dev : (b + 1) * tok_dev] = jnp.max(hits, axis=0, keepdims=True)
    hidden_width = weight_ref.shape[0] // 2
    step_rows = gram_step(hidden_width)
    mask = mask_ref[0:1, :]

    def step(j, _):
        at = pl.multiple_of(j * step_rows, step_rows)
        gate = lax.dot_general(
            weight_ref[pl.ds(at, step_rows), :], x_ref[...], NT, preferred_element_type=F32
        )
        up = lax.dot_general(
            weight_ref[pl.ds(pl.multiple_of(at + hidden_width, step_rows), step_rows), :],
            x_ref[...],
            NT,
            preferred_element_type=F32,
        )
        hidden_ref[pl.ds(at, step_rows), :] = (gate / (1.0 + jnp.exp(-gate)) * up * mask).astype(BF16)
        return 0

    lax.fori_loop(0, hidden_width // step_rows, step, 0)
    for first in range(0, hidden_width, step_rows):
        product = lax.dot_general(
            hidden_ref[first : first + step_rows, :],
            hidden_ref[first:, :],
            NT,
            preferred_element_type=F32,
        )
        if has_gram:
            product += gram_in[first : first + step_rows, first:]
        if scale is not None:
            product *= scale
            for a in range(first // LANES, (first + step_rows) // LANES):
                for b in range(a, hidden_width // LANES):
                    at = upper_tiles(hidden_width // LANES).index((a, b)) * LANES
                    row, column = a * LANES - first, b * LANES - first
                    packed_out[at : at + LANES, :] = product[
                        row : row + LANES, column : column + LANES
                    ].astype(BF16)
        gram_out[first : first + step_rows, first:] = product


def ffn(expert, weight_t, pieces, sources, gram, tok_dev, scale=None):
    hidden_width, width = weight_t.shape[0] // 2, weight_t.shape[1]
    rows = tok_dev * len(sources)
    out_shape = [jax.ShapeDtypeStruct((hidden_width, hidden_width), F32)]
    if scale is not None:
        packed = len(upper_tiles(hidden_width // LANES)) * LANES
        out_shape.append(jax.ShapeDtypeStruct((packed, LANES), BF16))
    operands = [expert, weight_t, *pieces] + ([] if gram is None else [gram])
    return pl.pallas_call(
        functools.partial(
            ffn_kernel,
            tok_dev=tok_dev,
            width=width,
            sources=sources,
            has_gram=gram is not None,
            scale=scale,
        ),
        out_shape=out_shape,
        in_specs=[SMEM] + [VMEM] * (len(operands) - 1),
        out_specs=[VMEM] * len(out_shape),
        scratch_shapes=[
            pltpu.VMEM((rows, width), BF16),
            pltpu.VMEM((8, rows), F32),
            pltpu.VMEM((hidden_width, rows), BF16),
        ],
        compiler_params=params(16),
        cost_estimate=pl.CostEstimate(
            flops=2 * rows * hidden_width * (2 * width + hidden_width),
            bytes_accessed=weight_t.size * 2 + rows * width * 2,
            transcendentals=rows * hidden_width,
        ),
    )(*operands)


def power_kernel(*refs, has_other):
    if has_other:
        group_ref, own_ref, other_ref, reduced_ref, w_ref, wt_ref = refs[:6]
        rest = refs[6:]
    else:
        group_ref, own_ref, reduced_ref, w_ref, wt_ref = refs[:5]
        rest = refs[5:]
    gram_ref, power_ref, full_ref, high_ref, low_ref, probe_ref = rest
    tiles = full_ref.shape[0] // LANES
    for at, (a, b) in enumerate(upper_tiles(tiles)):
        rows, columns = slice(a * LANES, (a + 1) * LANES), slice(b * LANES, (b + 1) * LANES)
        tile = own_ref[rows, columns]
        if has_other:
            tile += other_ref[at * LANES : (at + 1) * LANES, :].astype(F32)
        full_ref[rows, columns] = tile
        if a != b:
            full_ref[columns, rows] = tile.T
    group = group_ref[0]
    panel_rows = gram_ref.shape[0]
    gram_ref[...] = full_ref[pl.ds(pl.multiple_of(group * panel_rows, panel_rows), panel_rows), :]
    full = full_ref[...]
    high = full.astype(BF16)
    high_ref[...] = high
    low_ref[...] = (full - high.astype(F32)).astype(BF16)

    def panel_of(reduced):
        high = reduced.astype(BF16)
        low = (reduced - high.astype(F32)).astype(BF16)
        total = jnp.dot(low_ref[...], high, preferred_element_type=F32)
        total += jnp.dot(high_ref[...], low, preferred_element_type=F32)
        total += jnp.dot(high_ref[...], high, preferred_element_type=F32)
        return total.astype(BF16)

    image = jnp.dot(w_ref[...], panel_of(reduced_ref[...]), preferred_element_type=F32)
    mean = jnp.sum(image * image, axis=0, keepdims=True) * (1.0 / image.shape[0])
    probe_ref[...] = (image * lax.rsqrt(mean + 1e-06)).astype(BF16)
    panel = panel_of(jnp.dot(wt_ref[...], probe_ref[...], preferred_element_type=F32))
    own_rows = power_ref.shape[0]
    power_ref[...] = jnp.dot(
        w_ref[pl.ds(pl.multiple_of(group * own_rows, own_rows), own_rows), :],
        panel,
        preferred_element_type=F32,
    )


def power(group, own, other, reduced, w_down, w_down_t, group_count):
    width, hidden_width = w_down.shape
    rank = reduced.shape[1]
    operands = [group, own] + ([] if other is None else [other]) + [reduced, w_down, w_down_t]
    return pl.pallas_call(
        functools.partial(power_kernel, has_other=other is not None),
        out_shape=(
            jax.ShapeDtypeStruct((hidden_width // group_count, hidden_width), F32),
            jax.ShapeDtypeStruct((width // group_count, rank), F32),
        ),
        in_specs=[SMEM] + [VMEM] * (len(operands) - 1),
        out_specs=(VMEM, VMEM),
        scratch_shapes=[
            pltpu.VMEM((hidden_width, hidden_width), F32),
            pltpu.VMEM((hidden_width, hidden_width), BF16),
            pltpu.VMEM((hidden_width, hidden_width), BF16),
            pltpu.VMEM((width, rank), BF16),
        ],
        compiler_params=params(24),
        cost_estimate=pl.CostEstimate(
            flops=2 * rank * (6 * hidden_width * hidden_width + 3 * width * hidden_width),
            bytes_accessed=w_down.size * 8,
            transcendentals=0,
        ),
    )(*operands)


def whole(rows, at_operand):
    return ((at_operand, 0), (at_operand, rows))


def gathered_in_steps(block, weights, expert, tok_dev, scale, depth):
    per_chip = 2
    per_row = 2 * per_chip
    index = lax.axis_index("expert")
    place = index // per_row
    inner = (place == 1) | (place == 2)
    rows = block.shape[0] // 2

    def line(pairs):
        return [(a * per_row + r, b * per_row + r) for a, b in pairs for r in range(per_row)]

    ends_swap = line([(0, 1), (1, 0), (2, 3), (3, 2)])
    middle_swap = line([(1, 2), (2, 1)])
    outward = line([(1, 0), (2, 3)])
    inward = line([(0, 1), (3, 2)])
    across = [(i, i ^ per_chip) for i in range(depth * per_row)]
    sibling = [(i, i ^ 1) for i in range(depth * per_row)]

    def send(array, pairs):
        return lax.ppermute(array, "expert", pairs)

    def run(pieces, sources, gram, scale=None):
        return ffn(expert, weights, pieces, sources, gram, tok_dev, scale)

    pair = lambda *arrays: [whole(rows, i) for i in range(len(arrays))]

    q1 = send(block, ends_swap)
    q2 = send(block, middle_swap)
    y0 = send(block, across)
    block_s = send(block, sibling)
    gram = run([block, block_s], pair(block, block_s), None)[0]

    y1 = send(q1, across)
    p1 = send(q1, middle_swap)
    p2 = send(q2, outward)
    far1 = send(y0[rows:], inward)
    q1_s = send(q1, sibling)
    y0_s = send(y0, sibling)
    pieces = [q1, y0, q1_s, y0_s]
    gram = run(pieces, pair(*pieces), gram)[0]

    r2 = jnp.where(inner, q2, p2)
    y2 = send(r2, across)
    p3 = send(p1, outward)
    far2 = send(far1, middle_swap)
    r2_s = send(r2, sibling)
    y1_s = send(y1, sibling)
    pieces = [r2, y1, r2_s, y1_s]
    gram = run(pieces, pair(*pieces), gram)[0]

    r3 = jnp.where(inner, p1, p3)
    y3 = send(r3[:rows], across)
    far3 = send(far2, outward)
    r3_s = send(r3, sibling)
    y2_s = send(y2, sibling)
    pieces = [r3, y2, r3_s, y2_s]
    gram = run(pieces, pair(*pieces), gram)[0]

    far = jnp.where(inner, far2, far3)
    y3_s = send(y3, sibling)
    far_s = send(far, sibling)
    return run(
        [y3, far, y3_s, far_s], [((0, 0), (1, 0)), ((2, 0), (3, 0))], gram, scale
    )


def gathered_whole(block, weights, expert, tok_dev, scale):
    rows = block.shape[0] // 2
    blocks = lax.all_gather(block, "expert", axis=0)
    count = blocks.shape[0]
    at_once = BLOCKS_PER_CALL if count % BLOCKS_PER_CALL == 0 else 1
    sources = [whole(rows, i) for i in range(at_once)]

    def step(i, gram):
        pieces = [
            lax.dynamic_index_in_dim(blocks, i * at_once + b, 0, keepdims=False)
            for b in range(at_once)
        ]
        return ffn(expert, weights, pieces, sources, gram, tok_dev)[0]

    hidden_width = weights.shape[0] // 2
    gram = lax.fori_loop(0, count // at_once, step, jnp.zeros((hidden_width, hidden_width), F32))
    return gram * scale


def on_device(tokens, routes, gate_up, down_weight, sketch):
    owner_count = lax.axis_size("expert")
    group_count = lax.axis_size("group")
    tok_dev = tokens.shape[1]
    depth = owner_count // (2 * group_count)
    stepwise = group_count == 2 and depth == 4 and owner_count == 2 * group_count * depth
    expert = lax.axis_index("expert").astype(jnp.int32)[None]
    group = lax.axis_index("group").astype(jnp.int32)[None]
    scale = 1.0 / (tok_dev * TOPK * group_count)
    block = pack(tokens[0], routes[0])
    weights = transposed(gate_up[0])
    w_down = down_weight[0]
    w_down_t, reduced = reduced_first(w_down, sketch[0])
    if stepwise:
        own, packed = gathered_in_steps(block, weights, expert, tok_dev, scale, depth)
        other = lax.ppermute(packed, "group", [(0, 1), (1, 0)])
    else:
        own = lax.psum(gathered_whole(block, weights, expert, tok_dev, scale), "group")
        other = None
    gram, result = power(group, own, other, reduced, w_down, w_down_t, group_count)
    return gram[None], result[None]


def solution(mesh):
    return jax.shard_map(
        on_device,
        mesh=mesh,
        in_specs=(
            P("group", "expert", None),
            P("group", "expert", None),
            P("expert", None, None),
            P("expert", None, None),
            P("expert", None, None),
        ),
        out_specs=(P("expert", "group", None), P("expert", "group", None)),
        check_vma=False,
    )
```

```python
import functools

import jax
import jax.numpy as jnp
from jax import lax
from jax.experimental import pallas as pl
from jax.experimental.pallas import tpu as pltpu
from jax.sharding import PartitionSpec as P

TOPK = 8
LANES = 128
ID_ROWS = 16
NT = (((1,), (1,)), ((), ()))
NN = (((1,), (0,)), ((), ()))
TN = (((0,), (0,)), ((), ()))
TT = (((0,), (1,)), ((), ()))
BF16 = jnp.bfloat16
F32 = jnp.float32
VMEM = pl.BlockSpec(memory_space=pltpu.VMEM)
MIB = 1 << 20


def here(array):
    return pltpu.with_memory_space_constraint(array, pltpu.VMEM)


def far(array):
    return pltpu.with_memory_space_constraint(array, pltpu.HBM)


def kept(shape, dtype):
    return pltpu.VMEM(tuple(shape), dtype)


def params(mib):
    return pltpu.CompilerParams(vmem_limit_bytes=mib * MIB)


def half_rows(tok_dev, width):
    return tok_dev // 2 * (width // LANES) + ID_ROWS


def pack_kernel(tokens_hbm, routes_hbm, out_ref, tokens_ref, routes_ref, sems):
    copies = [
        pltpu.make_async_copy(routes_hbm, routes_ref, sems.at[0]),
        pltpu.make_async_copy(tokens_hbm, tokens_ref, sems.at[1]),
    ]
    for copy in copies:
        copy.start()
    for copy in copies:
        copy.wait()
    tok_dev, width = tokens_ref.shape
    top = routes_ref.shape[0]
    half, tiles = tok_dev // 2, width // LANES
    rows = half_rows(tok_dev, width)
    ids = jnp.concatenate(
        [routes_ref[...].astype(F32), jnp.full((ID_ROWS - top, tok_dev), -1.0, F32)], axis=0
    )
    lane = lax.broadcasted_iota(jnp.int32, ids.shape, 1)
    for h in range(2):
        for i in range(half // 16):
            for k in range(tiles):
                at = h * rows + (i * tiles + k) * 16
                out_ref[at : at + 16, :] = tokens_ref[
                    h * half + i * 16 : h * half + (i + 1) * 16, k * LANES : (k + 1) * LANES
                ]
        mine = (lane >= h * half) & (lane < (h + 1) * half)
        out_ref[(h + 1) * rows - ID_ROWS : (h + 1) * rows, :tok_dev] = jnp.where(
            mine, ids, -1.0
        ).astype(BF16)


def pack(tokens, routes):
    tok_dev, width = tokens.shape
    anywhere = pl.BlockSpec(memory_space=pl.ANY)
    return pl.pallas_call(
        pack_kernel,
        out_shape=kept((2 * half_rows(tok_dev, width), LANES), BF16),
        in_specs=[anywhere, anywhere],
        out_specs=VMEM,
        scratch_shapes=[
            pltpu.VMEM(tokens.shape, tokens.dtype),
            pltpu.VMEM(routes.shape, routes.dtype),
            pltpu.SemaphoreType.DMA((2,)),
        ],
        compiler_params=params(2),
        cost_estimate=pl.CostEstimate(flops=0, bytes_accessed=tokens.size * 4, transcendentals=0),
    )(far(tokens), far(routes))


def split(value):
    high = value.astype(BF16)
    return high, (value - high.astype(F32)).astype(BF16)


def product(left, right, dims):
    return lax.dot_general(left, right, dims, preferred_element_type=F32)


def reduce_kernel(w_hbm, sketch_hbm, tie_ref, high_ref, low_ref, tie_out, w_ref, sketch_ref, sems):
    copies = [
        pltpu.make_async_copy(w_hbm, w_ref, sems.at[0]),
        pltpu.make_async_copy(sketch_hbm, sketch_ref, sems.at[1]),
    ]
    for copy in copies:
        copy.start()
    for copy in copies:
        copy.wait()
    high_ref[...], low_ref[...] = split(product(w_ref[...], sketch_ref[...], TN))
    tie_out[...] = jnp.zeros_like(tie_out)


def reduced_first(w_down, sketch, tie):
    half = kept((w_down.shape[1], sketch.shape[1]), BF16)
    anywhere = pl.BlockSpec(memory_space=pl.ANY)
    return pl.pallas_call(
        reduce_kernel,
        out_shape=(half, half, kept(tie.shape, tie.dtype)),
        in_specs=[anywhere, anywhere, VMEM],
        out_specs=(VMEM, VMEM, VMEM),
        scratch_shapes=[
            pltpu.VMEM(w_down.shape, w_down.dtype),
            pltpu.VMEM(sketch.shape, sketch.dtype),
            pltpu.SemaphoreType.DMA((2,)),
        ],
        compiler_params=params(6),
        cost_estimate=pl.CostEstimate(
            flops=2 * w_down.size * sketch.shape[1], bytes_accessed=w_down.size * 2, transcendentals=0
        ),
    )(far(w_down), far(sketch), here(tie))


def nothing_kernel(in_ref, tie_ref, out_ref):
    pass


def after(tie, array):
    return pl.pallas_call(
        nothing_kernel,
        out_shape=kept(array.shape, array.dtype),
        in_specs=[VMEM, VMEM],
        out_specs=VMEM,
        input_output_aliases={0: 0},
        compiler_params=params(2),
        cost_estimate=pl.CostEstimate(flops=0, bytes_accessed=0, transcendentals=0),
    )(here(array), here(tie))


def part_kernel(in_ref, out_ref, *, first):
    out_ref[...] = in_ref[first : first + out_ref.shape[0], :]


def part(array, first, rows):
    return pl.pallas_call(
        functools.partial(part_kernel, first=first),
        out_shape=kept((rows, array.shape[1]), array.dtype),
        in_specs=[VMEM],
        out_specs=VMEM,
        compiler_params=params(2),
        cost_estimate=pl.CostEstimate(flops=0, bytes_accessed=0, transcendentals=0),
    )(here(array))


def right_tiles(count):
    return [(a, b) for a in range(count) for b in range(a + 1, count)]


def packed_rows(count):
    return (len(right_tiles(count)) + (count + 1) // 2) * LANES + ID_ROWS


def tile_places():
    return (
        lax.broadcasted_iota(jnp.int32, (LANES, LANES), 0),
        lax.broadcasted_iota(jnp.int32, (LANES, LANES), 1),
    )


def gram_step(hidden_width):
    return 2 * LANES if hidden_width % (2 * LANES) == 0 else LANES


def pack_gram(gram_ref, packed_ref):
    count = gram_ref.shape[0] // LANES
    rights = right_tiles(count)

    def tile(a, b):
        return gram_ref[a * LANES : (a + 1) * LANES, b * LANES : (b + 1) * LANES]

    for at, (a, b) in enumerate(rights):
        packed_ref[at * LANES : (at + 1) * LANES, :] = tile(a, b).astype(BF16)
    row, column = tile_places()
    strip = jnp.zeros((ID_ROWS, LANES), F32)
    place = lax.broadcasted_iota(jnp.int32, strip.shape, 0)
    for pair in range((count + 1) // 2):
        at = (len(rights) + pair) * LANES
        both = tile(2 * pair, 2 * pair)
        if 2 * pair + 1 < count:
            second = tile(2 * pair + 1, 2 * pair + 1)
            diagonal = jnp.sum(jnp.where(row == column, second, 0.0), axis=0, keepdims=True)
            strip = jnp.where(place == pair, diagonal, strip)
            both = jnp.where(row <= column, both, second)
        packed_ref[at : at + LANES, :] = both.astype(BF16)
    at = (len(rights) + (count + 1) // 2) * LANES
    packed_ref[at : at + ID_ROWS, :] = strip.astype(BF16)


def unpack_gram(packed_ref, full_ref):
    count = full_ref.shape[0] // LANES
    rights = right_tiles(count)

    def put(a, b, value):
        full_ref[a * LANES : (a + 1) * LANES, b * LANES : (b + 1) * LANES] = value.astype(BF16)

    for at, (a, b) in enumerate(rights):
        value = packed_ref[at * LANES : (at + 1) * LANES, :]
        put(a, b, value)
        put(b, a, value.astype(F32).T)
    row, column = tile_places()
    at = (len(rights) + (count + 1) // 2) * LANES
    strip = packed_ref[at : at + ID_ROWS, :].astype(F32)
    for pair in range((count + 1) // 2):
        at = (len(rights) + pair) * LANES
        both = packed_ref[at : at + LANES, :].astype(F32)
        turned = both.T
        put(2 * pair, 2 * pair, jnp.where(row <= column, both, turned))
        if 2 * pair + 1 < count:
            second = jnp.where(row > column, both, turned)
            second = jnp.where(row == column, strip[pair : pair + 1, :], second)
            put(2 * pair + 1, 2 * pair + 1, second)


def ffn_kernel(*refs, tok_dev, width, sources, has_gram, scale):
    operands = 1 + max(max(first[0], second[0]) for first, second in sources)
    weight_ref, pieces = refs[0], refs[1 : 1 + operands]
    rest = list(refs[1 + operands :])
    gram_in = rest.pop(0) if has_gram else None
    gram_out = rest.pop(0)
    last_out = rest.pop(0)
    x_ref, mask_ref, hidden_ref = rest
    half, tiles = tok_dev // 2, width // LANES
    expert = lax.axis_index("expert").astype(F32)
    for b, block in enumerate(sources):
        hits = None
        for h, (operand, first) in enumerate(block):
            piece = pieces[operand]
            for i in range(half // 16):
                for k in range(tiles):
                    at = first + (i * tiles + k) * 16
                    row = b * tok_dev + h * half + i * 16
                    x_ref[row : row + 16, k * LANES : (k + 1) * LANES] = piece[at : at + 16, :]
            at = first + half * tiles
            found = (piece[at : at + ID_ROWS, :tok_dev].astype(F32) == expert).astype(F32)
            hits = found if hits is None else hits + found
        mask_ref[0:1, b * tok_dev : (b + 1) * tok_dev] = jnp.max(hits, axis=0, keepdims=True)
    hidden_width = weight_ref.shape[1] // 2
    step_rows = gram_step(hidden_width)

    gate = product(weight_ref[:, :hidden_width], x_ref[...], TT)
    up = product(weight_ref[:, hidden_width:], x_ref[...], TT)
    hidden_ref[...] = (gate / (1.0 + jnp.exp(-gate)) * up * mask_ref[0:1, :]).astype(BF16)
    for first in range(0, hidden_width, step_rows):
        rows = slice(first, first + step_rows)
        part = product(hidden_ref[rows, :], hidden_ref[first:, :], NT)
        if has_gram:
            part += gram_in[rows, first:]
        if scale is not None:
            part *= scale
        gram_out[rows, first:] = part
    if scale is not None:
        pack_gram(gram_out, last_out)
    else:
        last_out[...] = jnp.zeros_like(last_out)


def ffn(weights, pieces, sources, gram, tok_dev, scale=None):
    hidden_width, width = weights.shape[1] // 2, weights.shape[0]
    rows = tok_dev * len(sources)
    if scale is None:
        last = kept((8, LANES), F32)
    else:
        last = kept((packed_rows(hidden_width // LANES), LANES), BF16)
    operands = [weights, *pieces] + ([] if gram is None else [gram])
    return pl.pallas_call(
        functools.partial(
            ffn_kernel,
            tok_dev=tok_dev,
            width=width,
            sources=sources,
            has_gram=gram is not None,
            scale=scale,
        ),
        out_shape=(kept((hidden_width, hidden_width), F32), last),
        in_specs=[VMEM] * len(operands),
        out_specs=(VMEM, VMEM),
        input_output_aliases={} if gram is None else {len(operands) - 1: 0},
        scratch_shapes=[
            pltpu.VMEM((rows, width), BF16),
            pltpu.VMEM((8, rows), F32),
            pltpu.VMEM((hidden_width, rows), BF16),
        ],
        compiler_params=params(8),
        cost_estimate=pl.CostEstimate(
            flops=4 * rows * hidden_width * (2 * width + hidden_width),
            bytes_accessed=weights.size * 2 + rows * width * 2,
            transcendentals=rows * hidden_width,
        ),
    )(*map(here, operands))


def exact(high, low, other_high, other_low):
    total = product(low, other_high, NN)
    total += product(high, other_low, NN)
    return total + product(high, other_high, NN)


def own_kernel(own_ref, high_ref, low_ref, w_hbm, full_ref, panel_ref, w_ref, sem):
    copy = pltpu.make_async_copy(w_hbm, w_ref, sem)
    copy.start()
    count = own_ref.shape[0] // LANES
    for a in range(count):
        for b in range(a, count):
            rows, columns = slice(a * LANES, (a + 1) * LANES), slice(b * LANES, (b + 1) * LANES)
            tile = own_ref[rows, columns]
            full_ref[rows, columns] = tile
            if a != b:
                full_ref[columns, rows] = tile.T
    for first in range(0, own_ref.shape[0], 2 * LANES):
        rows = slice(first, min(first + 2 * LANES, own_ref.shape[0]))
        high, low = split(full_ref[rows, :])
        panel_ref[rows, :] = exact(high, low, high_ref[...], low_ref[...])
    copy.wait()


def own_side(own, high, low, w_down):
    hidden_width, rank = high.shape
    return pl.pallas_call(
        own_kernel,
        out_shape=(
            kept((hidden_width, hidden_width), F32),
            kept((hidden_width, rank), F32),
            kept(w_down.shape, w_down.dtype),
        ),
        in_specs=[VMEM] * 3 + [pl.BlockSpec(memory_space=pl.ANY)],
        out_specs=(VMEM, VMEM, VMEM),
        scratch_shapes=[pltpu.SemaphoreType.DMA],
        compiler_params=params(4),
        cost_estimate=pl.CostEstimate(
            flops=6 * hidden_width * hidden_width * rank,
            bytes_accessed=w_down.size * 2,
            transcendentals=0,
        ),
    )(here(own), here(high), here(low), far(w_down))


def power_kernel(*refs, has_other):
    refs = list(refs)
    own_ref, panel_ref = refs[:2]
    other_ref = refs.pop(2) if has_other else None
    first_high, first_low, w_ref, gram_out, power_out = refs[2:7]
    full_ref, other_full, high_ref, low_ref, image_ref, probe_ref, power_ref, sems = refs[7:]
    group = lax.axis_index("group")
    hidden_width = full_ref.shape[0]
    panel = panel_ref[...]
    if has_other:
        unpack_gram(other_ref, other_full)
        panel += product(other_full[...], first_low[...], NN)
        panel += product(other_full[...], first_high[...], NN)
    image_ref[...] = product(w_ref[...], panel.astype(BF16), NN)
    for first in range(0, hidden_width, LANES):
        rows = slice(first, first + LANES)
        full = own_ref[rows, :]
        if has_other:
            full += other_full[rows, :].astype(F32)
        full_ref[rows, :] = full
        high_ref[rows, :], low_ref[rows, :] = split(full)
    panel_rows = gram_out.shape[0]
    gram_copy = pltpu.make_async_copy(
        full_ref.at[pl.ds(pl.multiple_of(group * panel_rows, panel_rows), panel_rows), :],
        gram_out,
        sems.at[0],
    )
    gram_copy.start()
    image = image_ref[...]
    mean = jnp.sum(image * image, axis=0, keepdims=True) * (1.0 / image.shape[0])
    probe_ref[...] = (image * lax.rsqrt(mean + 1e-06)).astype(BF16)
    high, low = split(product(w_ref[...], probe_ref[...], TN))
    panel = exact(high_ref[...], low_ref[...], high, low).astype(BF16)
    own_rows = power_ref.shape[0]
    chunk = min(own_rows, 4 * LANES)
    copies = []
    for at, first in enumerate(range(0, own_rows, chunk)):
        rows = pl.ds(pl.multiple_of(group * own_rows + first, chunk), chunk)
        power_ref[first : first + chunk, :] = product(w_ref[rows, :], panel, NN)
        copies.append(
            pltpu.make_async_copy(
                power_ref.at[first : first + chunk, :],
                power_out.at[first : first + chunk, :],
                sems.at[1 + at],
            )
        )
        copies[-1].start()
    gram_copy.wait()
    for copy in copies:
        copy.wait()


def power(own, other, panel, reduced, w_down, group_count):
    width, hidden_width = w_down.shape
    rank = panel.shape[1]
    own_rows = width // group_count
    operands = [own, panel] + ([] if other is None else [other])
    operands += [*reduced, w_down]
    anywhere = pl.BlockSpec(memory_space=pl.ANY)
    return pl.pallas_call(
        functools.partial(power_kernel, has_other=other is not None),
        out_shape=(
            jax.ShapeDtypeStruct((hidden_width // group_count, hidden_width), F32),
            jax.ShapeDtypeStruct((own_rows, rank), F32),
        ),
        in_specs=[VMEM] * len(operands),
        out_specs=(anywhere, anywhere),
        scratch_shapes=[
            pltpu.VMEM((hidden_width, hidden_width), F32),
            pltpu.VMEM((hidden_width, hidden_width), BF16),
            pltpu.VMEM((hidden_width, hidden_width), BF16),
            pltpu.VMEM((hidden_width, hidden_width), BF16),
            pltpu.VMEM((width, rank), F32),
            pltpu.VMEM((width, rank), BF16),
            pltpu.VMEM((own_rows, rank), F32),
            pltpu.SemaphoreType.DMA((1 + own_rows // min(own_rows, 4 * LANES),)),
        ],
        compiler_params=params(12),
        cost_estimate=pl.CostEstimate(
            flops=2 * rank * (6 * hidden_width * hidden_width + 3 * width * hidden_width),
            bytes_accessed=w_down.size * 4,
            transcendentals=0,
        ),
    )(*map(here, operands))


def whole(rows, at_operand):
    return ((at_operand, 0), (at_operand, rows))


def ring_order(chips, across):
    depth = chips // across
    if across < 2 or depth % 2 or depth * across != chips:
        return list(range(chips))
    order = []
    for z in range(depth):
        row = range(1, across) if z % 2 == 0 else range(across - 1, 0, -1)
        order += [z * across + y for y in row]
    return order + [z * across for z in reversed(range(depth))]


def gram_of_all(block, weights, tok_dev, scale, order, prepare):
    chips, rows = len(order), block.shape[0] // 2
    onward = [
        (2 * order[i] + core, 2 * order[(i + 1) % chips] + core)
        for i in range(chips)
        for core in range(2)
    ]
    backward = [(b, a) for a, b in onward]
    sibling = [(i, i ^ 1) for i in range(2 * chips)]

    def send(array, pairs):
        return lax.ppermute(array, "expert", pairs)

    right = left = block
    pieces, gram, tie = [block], None, None
    for step in range(1, (chips + 1) // 2):
        if tie is not None:
            right, left = after(tie, right), after(tie, left)
            pieces = [right, left]
        next_right, next_left = send(right, onward), send(left, backward)
        pieces += [send(piece, sibling) for piece in pieces]
        sources = [whole(rows, i) for i in range(len(pieces))]
        gram, tie = ffn(weights, pieces, sources, gram, tok_dev)
        if step == 1:
            *reduced, tie = prepare(tie)
        right, left = next_right, next_left
    last = [((0, 0), (1, 0)), ((2, 0), (3, 0))]
    if chips % 2 == 0:
        pieces = [block]
        if tie is not None:
            right, left = after(tie, right), after(tie, left)
            pieces = [right, left]
        next_right = send(part(right, 0, rows), onward)
        next_left = send(part(left, rows, rows), backward)
        pieces += [send(piece, sibling) for piece in pieces]
        sources = [whole(rows, i) for i in range(len(pieces))]
        gram, tie = ffn(weights, pieces, sources, gram, tok_dev)
        right, left = after(tie, next_right), after(tie, next_left)
    else:
        last = [whole(rows, i) for i in range(4)]
    pieces = [right, left, send(right, sibling), send(left, sibling)]
    return *ffn(weights, pieces, last, gram, tok_dev, scale), reduced


def on_device(tokens, routes, gate_up, down_weight, sketch):
    owner_count = lax.axis_size("expert")
    group_count = lax.axis_size("group")
    tok_dev = tokens.shape[1]
    order = ring_order(owner_count // 2, group_count)
    scale = 1.0 / (tok_dev * TOPK * group_count)
    block = pack(tokens[0], routes[0].T)
    w_down = down_weight[0]
    own, packed, reduced = gram_of_all(
        block,
        gate_up[0],
        tok_dev,
        scale,
        order,
        functools.partial(reduced_first, w_down, sketch[0]),
    )
    if group_count == 2:
        other = lax.ppermute(packed, "group", [(0, 1), (1, 0)])
    else:
        own, other = lax.psum(own, "group"), None
    own, panel, w_down = own_side(own, *reduced, w_down)
    gram, result = power(own, other, panel, reduced, w_down, group_count)
    return gram[None], result[None]


def solution(mesh):
    return jax.shard_map(
        on_device,
        mesh=mesh,
        in_specs=(
            P("group", "expert", None),
            P("group", "expert", None),
            P("expert", None, None),
            P("expert", None, None),
            P("expert", None, None),
        ),
        out_specs=(P("expert", "group", None), P("expert", "group", None)),
        check_vma=False,
    )
```

```python
import functools

import jax
import jax.numpy as jnp
from jax import lax
from jax.experimental import pallas as pl
from jax.experimental.pallas import tpu as pltpu
from jax.sharding import PartitionSpec as P

TOPK = 8
LANES = 128
ID_ROWS = 16
NT = (((1,), (1,)), ((), ()))
NN = (((1,), (0,)), ((), ()))
TN = (((0,), (0,)), ((), ()))
TT = (((0,), (1,)), ((), ()))
BF16 = jnp.bfloat16
F32 = jnp.float32
VMEM = pl.BlockSpec(memory_space=pltpu.VMEM)
MIB = 1 << 20


def here(array):
    return pltpu.with_memory_space_constraint(array, pltpu.VMEM)


def far(array):
    return pltpu.with_memory_space_constraint(array, pltpu.HBM)


def kept(shape, dtype):
    return pltpu.VMEM(tuple(shape), dtype)


def params(mib):
    return pltpu.CompilerParams(vmem_limit_bytes=mib * MIB)


def half_rows(tok_dev, width):
    return tok_dev // 2 * (width // LANES) + ID_ROWS


def pack_kernel(tokens_hbm, routes_hbm, first_ref, second_ref, tokens_ref, routes_ref, sems):
    copies = [
        pltpu.make_async_copy(routes_hbm, routes_ref, sems.at[0]),
        pltpu.make_async_copy(tokens_hbm, tokens_ref, sems.at[1]),
    ]
    for copy in copies:
        copy.start()
    for copy in copies:
        copy.wait()
    tok_dev, width = tokens_ref.shape
    top = routes_ref.shape[0]
    half, tiles = tok_dev // 2, width // LANES
    rows = half_rows(tok_dev, width)
    ids = jnp.concatenate(
        [routes_ref[...].astype(F32), jnp.full((ID_ROWS - top, tok_dev), -1.0, F32)], axis=0
    )
    lane = lax.broadcasted_iota(jnp.int32, ids.shape, 1)
    for h, out_ref in enumerate((first_ref, second_ref)):
        for i in range(half // 16):
            for k in range(tiles):
                at = (i * tiles + k) * 16
                out_ref[at : at + 16, :] = tokens_ref[
                    h * half + i * 16 : h * half + (i + 1) * 16, k * LANES : (k + 1) * LANES
                ]
        mine = (lane >= h * half) & (lane < (h + 1) * half)
        out_ref[rows - ID_ROWS :, :tok_dev] = jnp.where(mine, ids, -1.0).astype(BF16)


def pack(tokens, routes):
    tok_dev, width = tokens.shape
    anywhere = pl.BlockSpec(memory_space=pl.ANY)
    return pl.pallas_call(
        pack_kernel,
        out_shape=(kept((half_rows(tok_dev, width), LANES), BF16),) * 2,
        in_specs=[anywhere, anywhere],
        out_specs=(VMEM, VMEM),
        scratch_shapes=[
            pltpu.VMEM(tokens.shape, tokens.dtype),
            pltpu.VMEM(routes.shape, routes.dtype),
            pltpu.SemaphoreType.DMA((2,)),
        ],
        compiler_params=params(2),
        cost_estimate=pl.CostEstimate(flops=0, bytes_accessed=tokens.size * 4, transcendentals=0),
    )(far(tokens), far(routes))


def split(value):
    high = value.astype(BF16)
    return high, (value - high.astype(F32)).astype(BF16)


def product(left, right, dims):
    return lax.dot_general(left, right, dims, preferred_element_type=F32)


def reduce_kernel(w_hbm, sketch_hbm, tie_ref, high_ref, low_ref, tie_out, w_ref, sketch_ref, sems):
    copies = [
        pltpu.make_async_copy(w_hbm, w_ref, sems.at[0]),
        pltpu.make_async_copy(sketch_hbm, sketch_ref, sems.at[1]),
    ]
    for copy in copies:
        copy.start()
    for copy in copies:
        copy.wait()
    high_ref[...], low_ref[...] = split(product(w_ref[...], sketch_ref[...], TN))
    tie_out[...] = jnp.zeros_like(tie_out)


def reduced_first(w_down, sketch, tie):
    half = kept((w_down.shape[1], sketch.shape[1]), BF16)
    anywhere = pl.BlockSpec(memory_space=pl.ANY)
    return pl.pallas_call(
        reduce_kernel,
        out_shape=(half, half, kept(tie.shape, tie.dtype)),
        in_specs=[anywhere, anywhere, VMEM],
        out_specs=(VMEM, VMEM, VMEM),
        scratch_shapes=[
            pltpu.VMEM(w_down.shape, w_down.dtype),
            pltpu.VMEM(sketch.shape, sketch.dtype),
            pltpu.SemaphoreType.DMA((2,)),
        ],
        compiler_params=params(6),
        cost_estimate=pl.CostEstimate(
            flops=1000, bytes_accessed=1000, transcendentals=0
        ),
    )(far(w_down), far(sketch), here(tie))


def nothing_kernel(*refs):
    pass


def after(tie, array, *others):
    operands = (array, tie, *others)
    return pl.pallas_call(
        nothing_kernel,
        out_shape=kept(array.shape, array.dtype),
        in_specs=[VMEM] * len(operands),
        out_specs=VMEM,
        input_output_aliases={0: 0},
        compiler_params=params(2),
        cost_estimate=pl.CostEstimate(flops=1000, bytes_accessed=1000, transcendentals=0),
    )(*map(here, operands))


def right_tiles(count):
    return [(a, b) for a in range(count) for b in range(a + 1, count)]


def packed_rows(count):
    return (len(right_tiles(count)) + (count + 1) // 2) * LANES + ID_ROWS


def tile_places():
    return (
        lax.broadcasted_iota(jnp.int32, (LANES, LANES), 0),
        lax.broadcasted_iota(jnp.int32, (LANES, LANES), 1),
    )


def gram_step(hidden_width):
    return 2 * LANES if hidden_width % (2 * LANES) == 0 else LANES


def pack_gram(gram_ref, packed_ref):
    count = gram_ref.shape[0] // LANES
    rights = right_tiles(count)

    def tile(a, b):
        return gram_ref[a * LANES : (a + 1) * LANES, b * LANES : (b + 1) * LANES]

    for at, (a, b) in enumerate(rights):
        packed_ref[at * LANES : (at + 1) * LANES, :] = tile(a, b).astype(BF16)
    row, column = tile_places()
    strip = jnp.zeros((ID_ROWS, LANES), F32)
    place = lax.broadcasted_iota(jnp.int32, strip.shape, 0)
    for pair in range((count + 1) // 2):
        at = (len(rights) + pair) * LANES
        both = tile(2 * pair, 2 * pair)
        if 2 * pair + 1 < count:
            second = tile(2 * pair + 1, 2 * pair + 1)
            diagonal = jnp.sum(jnp.where(row == column, second, 0.0), axis=0, keepdims=True)
            strip = jnp.where(place == pair, diagonal, strip)
            both = jnp.where(row <= column, both, second)
        packed_ref[at : at + LANES, :] = both.astype(BF16)
    at = (len(rights) + (count + 1) // 2) * LANES
    packed_ref[at : at + ID_ROWS, :] = strip.astype(BF16)


def upper_tiles(count):
    return [(a, b) for a in range(count) for b in range(a, count)]


def tiles_of(gram_ref):
    for at, (a, b) in enumerate(upper_tiles(gram_ref.shape[0] // LANES)):
        yield (
            slice(at * LANES, (at + 1) * LANES),
            slice(a * LANES, (a + 1) * LANES),
            slice(b * LANES, (b + 1) * LANES),
        )


def unpack_gram(packed_ref, full_ref):
    count = full_ref.shape[0] // LANES
    rights = right_tiles(count)

    def put(a, b, value):
        full_ref[a * LANES : (a + 1) * LANES, b * LANES : (b + 1) * LANES] = value.astype(BF16)

    for at, (a, b) in enumerate(rights):
        value = packed_ref[at * LANES : (at + 1) * LANES, :]
        put(a, b, value)
        put(b, a, value.astype(F32).T)
    row, column = tile_places()
    at = (len(rights) + (count + 1) // 2) * LANES
    strip = packed_ref[at : at + ID_ROWS, :].astype(F32)
    for pair in range((count + 1) // 2):
        at = (len(rights) + pair) * LANES
        both = packed_ref[at : at + LANES, :].astype(F32)
        turned = both.T
        put(2 * pair, 2 * pair, jnp.where(row <= column, both, turned))
        if 2 * pair + 1 < count:
            second = jnp.where(row > column, both, turned)
            second = jnp.where(row == column, strip[pair : pair + 1, :], second)
            put(2 * pair + 1, 2 * pair + 1, second)


def ffn_kernel(*refs, tok_dev, width, operands, has_gram, has_tiles, for_sibling, gives, scale):
    weight_ref, pieces = refs[0], refs[1 : 1 + operands]
    rest = list(refs[1 + operands :])
    gram_in = rest.pop(0) if has_gram else None
    tiles_in = rest.pop(0) if has_tiles else None
    gram_out, last_out, x_ref, mask_ref, hidden_ref = rest[-5:]
    half, tiles = tok_dev // 2, width // LANES
    expert = lax.axis_index("expert")
    if for_sibling:
        expert = expert + 1 - 2 * (expert % 2)
    expert = expert.astype(F32)
    for b in range(operands // 2):
        hits = None
        for h in range(2):
            piece = pieces[2 * b + h]
            for i in range(half // 16):
                for k in range(tiles):
                    at = (i * tiles + k) * 16
                    row = b * tok_dev + h * half + i * 16
                    x_ref[row : row + 16, k * LANES : (k + 1) * LANES] = piece[at : at + 16, :]
            at = half * tiles
            found = (piece[at : at + ID_ROWS, :tok_dev].astype(F32) == expert).astype(F32)
            hits = found if hits is None else hits + found
        mask_ref[0:1, b * tok_dev : (b + 1) * tok_dev] = jnp.max(hits, axis=0, keepdims=True)
    hidden_width = weight_ref.shape[1] // 2
    step_rows = gram_step(hidden_width)

    gate = product(weight_ref[:, :hidden_width], x_ref[...], TT)
    up = product(weight_ref[:, hidden_width:], x_ref[...], TT)
    hidden_ref[...] = (gate / (1.0 + jnp.exp(-gate)) * up * mask_ref[0:1, :]).astype(BF16)
    for first in range(0, hidden_width, step_rows):
        rows = slice(first, first + step_rows)
        part = product(hidden_ref[rows, :], hidden_ref[first:, :], NT)
        if has_gram:
            part += gram_in[rows, first:]
        gram_out[rows, first:] = part if tiles_in is not None else part * scale
    if tiles_in is not None:
        for at, rows, columns in tiles_of(gram_out):
            gram_out[rows, columns] = (gram_out[rows, columns] + tiles_in[at, :]) * scale
    if gives == "packed":
        pack_gram(gram_out, last_out)
    elif gives == "tiles":
        for at, rows, columns in tiles_of(gram_out):
            last_out[at, :] = gram_out[rows, columns]
    else:
        last_out[...] = jnp.zeros_like(last_out)


def ffn(
    weights,
    pieces,
    gram,
    tok_dev,
    tiles=None,
    for_sibling=False,
    gives="tie",
    scale=1.0,
    wait=(),
    hides=False,
):
    hidden_width, width = weights.shape[1] // 2, weights.shape[0]
    count = hidden_width // LANES
    rows = tok_dev * len(pieces) // 2
    last = {
        "tie": kept((8, LANES), F32),
        "tiles": kept((len(upper_tiles(count)) * LANES, LANES), F32),
        "packed": kept((packed_rows(count), LANES), BF16),
    }[gives]
    more = [array for array in (gram, tiles) if array is not None]
    operands = [weights, *pieces, *more, *wait]
    return pl.pallas_call(
        functools.partial(
            ffn_kernel,
            tok_dev=tok_dev,
            width=width,
            operands=len(pieces),
            has_gram=gram is not None,
            has_tiles=tiles is not None,
            for_sibling=for_sibling,
            gives=gives,
            scale=scale,
        ),
        out_shape=(kept((hidden_width, hidden_width), F32), last),
        in_specs=[VMEM] * len(operands),
        out_specs=(VMEM, VMEM),
        input_output_aliases={} if gram is None else {1 + len(pieces): 0},
        scratch_shapes=[
            pltpu.VMEM((rows, width), BF16),
            pltpu.VMEM((8, rows), F32),
            pltpu.VMEM((hidden_width, rows), BF16),
        ],
        compiler_params=params(8),
        cost_estimate=pl.CostEstimate(
            flops=10**11 if hides else 1000,
            bytes_accessed=1000,
            transcendentals=0,
        ),
    )(*map(here, operands))


def exact(high, low, other_high, other_low):
    total = product(low, other_high, NN)
    total += product(high, other_low, NN)
    return total + product(high, other_high, NN)


def own_kernel(own_ref, high_ref, low_ref, w_hbm, full_ref, panel_ref, w_ref, sem):
    copy = pltpu.make_async_copy(w_hbm, w_ref, sem)
    copy.start()
    count = own_ref.shape[0] // LANES
    for a in range(count):
        for b in range(a, count):
            rows, columns = slice(a * LANES, (a + 1) * LANES), slice(b * LANES, (b + 1) * LANES)
            tile = own_ref[rows, columns]
            full_ref[rows, columns] = tile
            if a != b:
                full_ref[columns, rows] = tile.T
    for first in range(0, own_ref.shape[0], 2 * LANES):
        rows = slice(first, min(first + 2 * LANES, own_ref.shape[0]))
        high, low = split(full_ref[rows, :])
        panel_ref[rows, :] = exact(high, low, high_ref[...], low_ref[...])
    copy.wait()


def own_side(own, high, low, w_down):
    hidden_width, rank = high.shape
    return pl.pallas_call(
        own_kernel,
        out_shape=(
            kept((hidden_width, hidden_width), F32),
            kept((hidden_width, rank), F32),
            kept(w_down.shape, w_down.dtype),
        ),
        in_specs=[VMEM] * 3 + [pl.BlockSpec(memory_space=pl.ANY)],
        out_specs=(VMEM, VMEM, VMEM),
        scratch_shapes=[pltpu.SemaphoreType.DMA],
        compiler_params=params(4),
        cost_estimate=pl.CostEstimate(
            flops=6 * hidden_width * hidden_width * rank,
            bytes_accessed=w_down.size * 2,
            transcendentals=0,
        ),
    )(here(own), here(high), here(low), far(w_down))


def power_kernel(*refs, has_other):
    refs = list(refs)
    own_ref, panel_ref = refs[:2]
    other_ref = refs.pop(2) if has_other else None
    first_high, first_low, w_ref, gram_out, power_out = refs[2:7]
    full_ref, other_full, high_ref, low_ref, image_ref, probe_ref, power_ref, sems = refs[7:]
    group = lax.axis_index("group")
    hidden_width = full_ref.shape[0]
    panel = panel_ref[...]
    if has_other:
        unpack_gram(other_ref, other_full)
        panel += product(other_full[...], first_low[...], NN)
        panel += product(other_full[...], first_high[...], NN)
    image_ref[...] = product(w_ref[...], panel.astype(BF16), NN)
    for first in range(0, hidden_width, LANES):
        rows = slice(first, first + LANES)
        full = own_ref[rows, :]
        if has_other:
            full += other_full[rows, :].astype(F32)
        full_ref[rows, :] = full
        high_ref[rows, :], low_ref[rows, :] = split(full)
    panel_rows = gram_out.shape[0]
    gram_copy = pltpu.make_async_copy(
        full_ref.at[pl.ds(pl.multiple_of(group * panel_rows, panel_rows), panel_rows), :],
        gram_out,
        sems.at[0],
    )
    gram_copy.start()
    image = image_ref[...]
    mean = jnp.sum(image * image, axis=0, keepdims=True) * (1.0 / image.shape[0])
    probe_ref[...] = (image * lax.rsqrt(mean + 1e-06)).astype(BF16)
    high, low = split(product(w_ref[...], probe_ref[...], TN))
    panel = exact(high_ref[...], low_ref[...], high, low).astype(BF16)
    own_rows = power_ref.shape[0]
    chunk = min(own_rows, 4 * LANES)
    copies = []
    for at, first in enumerate(range(0, own_rows, chunk)):
        rows = pl.ds(pl.multiple_of(group * own_rows + first, chunk), chunk)
        power_ref[first : first + chunk, :] = product(w_ref[rows, :], panel, NN)
        copies.append(
            pltpu.make_async_copy(
                power_ref.at[first : first + chunk, :],
                power_out.at[first : first + chunk, :],
                sems.at[1 + at],
            )
        )
        copies[-1].start()
    gram_copy.wait()
    for copy in copies:
        copy.wait()


def power(own, other, panel, reduced, w_down, group_count):
    width, hidden_width = w_down.shape
    rank = panel.shape[1]
    own_rows = width // group_count
    operands = [own, panel] + ([] if other is None else [other])
    operands += [*reduced, w_down]
    anywhere = pl.BlockSpec(memory_space=pl.ANY)
    return pl.pallas_call(
        functools.partial(power_kernel, has_other=other is not None),
        out_shape=(
            jax.ShapeDtypeStruct((hidden_width // group_count, hidden_width), F32),
            jax.ShapeDtypeStruct((own_rows, rank), F32),
        ),
        in_specs=[VMEM] * len(operands),
        out_specs=(anywhere, anywhere),
        scratch_shapes=[
            pltpu.VMEM((hidden_width, hidden_width), F32),
            pltpu.VMEM((hidden_width, hidden_width), BF16),
            pltpu.VMEM((hidden_width, hidden_width), BF16),
            pltpu.VMEM((hidden_width, hidden_width), BF16),
            pltpu.VMEM((width, rank), F32),
            pltpu.VMEM((width, rank), BF16),
            pltpu.VMEM((own_rows, rank), F32),
            pltpu.SemaphoreType.DMA((1 + own_rows // min(own_rows, 4 * LANES),)),
        ],
        compiler_params=params(12),
        cost_estimate=pl.CostEstimate(
            flops=2 * rank * (6 * hidden_width * hidden_width + 3 * width * hidden_width),
            bytes_accessed=w_down.size * 4,
            transcendentals=0,
        ),
    )(*map(here, operands))


def ring_order(chips, across):
    depth = chips // across
    if across < 2 or depth % 2 or depth * across != chips:
        return list(range(chips))
    order = []
    for z in range(depth):
        row = range(1, across) if z % 2 == 0 else range(across - 1, 0, -1)
        order += [z * across + y for y in row]
    return order + [z * across for z in reversed(range(depth))]


def gram_of_all(halves, weights, tok_dev, scale, order, prepare):
    chips = len(order)
    onward = [
        (2 * order[i] + core, 2 * order[(i + 1) % chips] + core)
        for i in range(chips)
        for core in range(2)
    ]
    backward = [(b, a) for a, b in onward]
    sibling = [(i, i ^ 1) for i in range(2 * chips)]

    def send(array, pairs):
        return lax.ppermute(array, "expert", pairs)

    def swap(pieces):
        return [send(piece, sibling) for piece in pieces]

    slots = chips - 1
    weights_s = send(weights, sibling)
    sent = {s: (send(halves[s - 1], onward), send(halves[2 - s], backward)) for s in (1, 2) if s <= slots}
    *reduced, tie = prepare(jnp.zeros((8, LANES), F32))
    blocks, mine, others, tiles, pair = [halves], None, None, None, []
    for s in range(1, slots + 1):
        came = [after(tie, array) for array in sent[s]]
        if s + 2 <= slots:
            sent[s + 2] = (send(came[0], onward), send(came[1], backward))
        blocks.append(came if s % 2 else came[::-1])
        if s == slots:
            before = [after(came[0], array) for array in blocks[s - 1]]
            pieces = [*swap(blocks[s]), *swap(before)]
            mine, tie = ffn(weights, [*blocks[s], *before], mine, tok_dev, hides=True)
            return *ffn(weights, pieces, mine, tok_dev, tiles, gives="packed", scale=scale), reduced
        if s == slots - 1:
            if others is not None:
                tiles = send(tie, sibling)
            if pair:
                mine, tie = ffn(weights, pair, mine, tok_dev, wait=came)
            continue
        if s % 2:
            pair = [*blocks[s - 1], *blocks[s]]
        if s == slots - 2 or s % 2 == 0:
            others, tie = ffn(
                weights_s,
                pair,
                others,
                tok_dev,
                for_sibling=True,
                gives="tiles" if s == slots - 2 else "tie",
                wait=came,
            )
        else:
            mine, tie = ffn(weights, pair, mine, tok_dev, wait=came)
        if s % 2 == 0:
            pair = []


def on_device(tokens, routes, gate_up, down_weight, sketch):
    owner_count = lax.axis_size("expert")
    group_count = lax.axis_size("group")
    tok_dev = tokens.shape[1]
    order = ring_order(owner_count // 2, group_count)
    scale = 1.0 / (tok_dev * TOPK * group_count)
    halves = pack(tokens[0], routes[0].T)
    w_down = down_weight[0]
    own, packed, reduced = gram_of_all(
        halves,
        gate_up[0],
        tok_dev,
        scale,
        order,
        functools.partial(reduced_first, w_down, sketch[0]),
    )
    if group_count == 2:
        other = lax.ppermute(packed, "group", [(0, 1), (1, 0)])
    else:
        own, other = lax.psum(own, "group"), None
    own, panel, w_down = own_side(own, *reduced, w_down)
    gram, result = power(own, other, panel, reduced, w_down, group_count)
    return gram[None], result[None]


def solution(mesh):
    return jax.shard_map(
        on_device,
        mesh=mesh,
        in_specs=(
            P("group", "expert", None),
            P("group", "expert", None),
            P("expert", None, None),
            P("expert", None, None),
            P("expert", None, None),
        ),
        out_specs=(P("expert", "group", None), P("expert", "group", None)),
        check_vma=False,
    )
```

```python
import functools

import jax
import jax.numpy as jnp
from jax import lax
from jax.experimental import pallas as pl
from jax.experimental.pallas import tpu as pltpu
from jax.sharding import PartitionSpec as P

TOPK = 8
LANES = 128
ID_ROWS = 16
NT = (((1,), (1,)), ((), ()))
NN = (((1,), (0,)), ((), ()))
TN = (((0,), (0,)), ((), ()))
TT = (((0,), (1,)), ((), ()))
BF16 = jnp.bfloat16
F32 = jnp.float32
VMEM = pl.BlockSpec(memory_space=pltpu.VMEM)
MIB = 1 << 20


def here(array):
    return pltpu.with_memory_space_constraint(array, pltpu.VMEM)


def far(array):
    return pltpu.with_memory_space_constraint(array, pltpu.HBM)


def kept(shape, dtype):
    return pltpu.VMEM(tuple(shape), dtype)


def params(mib):
    return pltpu.CompilerParams(vmem_limit_bytes=mib * MIB)


def half_rows(tok_dev, width):
    return tok_dev // 2 * (width // LANES) + ID_ROWS


def pack_kernel(tokens_hbm, routes_hbm, first_ref, second_ref, tokens_ref, routes_ref, sems):
    copies = [
        pltpu.make_async_copy(routes_hbm, routes_ref, sems.at[0]),
        pltpu.make_async_copy(tokens_hbm, tokens_ref, sems.at[1]),
    ]
    for copy in copies:
        copy.start()
    for copy in copies:
        copy.wait()
    tok_dev, width = tokens_ref.shape
    top = routes_ref.shape[0]
    half, tiles = tok_dev // 2, width // LANES
    rows = half_rows(tok_dev, width)
    ids = jnp.concatenate(
        [routes_ref[...].astype(F32), jnp.full((ID_ROWS - top, tok_dev), -1.0, F32)], axis=0
    )
    lane = lax.broadcasted_iota(jnp.int32, ids.shape, 1)
    for h, out_ref in enumerate((first_ref, second_ref)):
        for i in range(half // 16):
            for k in range(tiles):
                at = (i * tiles + k) * 16
                out_ref[at : at + 16, :] = tokens_ref[
                    h * half + i * 16 : h * half + (i + 1) * 16, k * LANES : (k + 1) * LANES
                ]
        mine = (lane >= h * half) & (lane < (h + 1) * half)
        out_ref[rows - ID_ROWS :, :tok_dev] = jnp.where(mine, ids, -1.0).astype(BF16)


def pack(tokens, routes):
    tok_dev, width = tokens.shape
    anywhere = pl.BlockSpec(memory_space=pl.ANY)
    return pl.pallas_call(
        pack_kernel,
        out_shape=(kept((half_rows(tok_dev, width), LANES), BF16),) * 2,
        in_specs=[anywhere, anywhere],
        out_specs=(VMEM, VMEM),
        scratch_shapes=[
            pltpu.VMEM(tokens.shape, tokens.dtype),
            pltpu.VMEM(routes.shape, routes.dtype),
            pltpu.SemaphoreType.DMA((2,)),
        ],
        compiler_params=params(2),
        cost_estimate=pl.CostEstimate(flops=0, bytes_accessed=tokens.size * 4, transcendentals=0),
    )(far(tokens), far(routes))


def split(value):
    high = value.astype(BF16)
    return high, (value - high.astype(F32)).astype(BF16)


def product(left, right, dims):
    return lax.dot_general(left, right, dims, preferred_element_type=F32)


def reduce_kernel(w_hbm, sketch_hbm, *refs):
    *halves, high_ref, low_ref = refs[:4]
    *again, w_ref, sketch_ref, sems = refs[4:]
    copies = [
        pltpu.make_async_copy(w_hbm, w_ref, sems.at[0]),
        pltpu.make_async_copy(sketch_hbm, sketch_ref, sems.at[1]),
    ]
    for copy in copies:
        copy.start()
    for copy in copies:
        copy.wait()
    high_ref[...], low_ref[...] = split(product(w_ref[...], sketch_ref[...], TN))
    for half, copied in zip(halves, again):
        copied[...] = half[...]


def reduced_first(w_down, sketch, halves):
    half = kept((w_down.shape[1], sketch.shape[1]), BF16)
    anywhere = pl.BlockSpec(memory_space=pl.ANY)
    return pl.pallas_call(
        reduce_kernel,
        out_shape=(half, half, *(kept(array.shape, array.dtype) for array in halves)),
        in_specs=[anywhere, anywhere, VMEM, VMEM],
        out_specs=(VMEM,) * 4,
        scratch_shapes=[
            pltpu.VMEM(w_down.shape, w_down.dtype),
            pltpu.VMEM(sketch.shape, sketch.dtype),
            pltpu.SemaphoreType.DMA((2,)),
        ],
        compiler_params=params(6),
        cost_estimate=pl.CostEstimate(flops=10**11, bytes_accessed=1000, transcendentals=0),
    )(far(w_down), far(sketch), *map(here, halves))


def nothing_kernel(*refs):
    pass


def after(tie, array, *others):
    operands = (array, tie, *others)
    return pl.pallas_call(
        nothing_kernel,
        out_shape=kept(array.shape, array.dtype),
        in_specs=[VMEM] * len(operands),
        out_specs=VMEM,
        input_output_aliases={0: 0},
        compiler_params=params(2),
        cost_estimate=pl.CostEstimate(flops=1000, bytes_accessed=1000, transcendentals=0),
    )(*map(here, operands))


def right_tiles(count):
    return [(a, b) for a in range(count) for b in range(a + 1, count)]


def packed_rows(count):
    return (len(right_tiles(count)) + (count + 1) // 2) * LANES + ID_ROWS


def tile_places():
    return (
        lax.broadcasted_iota(jnp.int32, (LANES, LANES), 0),
        lax.broadcasted_iota(jnp.int32, (LANES, LANES), 1),
    )


def gram_step(hidden_width):
    return 2 * LANES if hidden_width % (2 * LANES) == 0 else LANES


def pack_gram(gram_ref, packed_ref):
    count = gram_ref.shape[0] // LANES
    rights = right_tiles(count)

    def tile(a, b):
        return gram_ref[a * LANES : (a + 1) * LANES, b * LANES : (b + 1) * LANES]

    for at, (a, b) in enumerate(rights):
        packed_ref[at * LANES : (at + 1) * LANES, :] = tile(a, b).astype(BF16)
    row, column = tile_places()
    strip = jnp.zeros((ID_ROWS, LANES), F32)
    place = lax.broadcasted_iota(jnp.int32, strip.shape, 0)
    for pair in range((count + 1) // 2):
        at = (len(rights) + pair) * LANES
        both = tile(2 * pair, 2 * pair)
        if 2 * pair + 1 < count:
            second = tile(2 * pair + 1, 2 * pair + 1)
            diagonal = jnp.sum(jnp.where(row == column, second, 0.0), axis=0, keepdims=True)
            strip = jnp.where(place == pair, diagonal, strip)
            both = jnp.where(row <= column, both, second)
        packed_ref[at : at + LANES, :] = both.astype(BF16)
    at = (len(rights) + (count + 1) // 2) * LANES
    packed_ref[at : at + ID_ROWS, :] = strip.astype(BF16)


def upper_tiles(count):
    return [(a, b) for a in range(count) for b in range(a, count)]


def tiles_of(gram_ref):
    for at, (a, b) in enumerate(upper_tiles(gram_ref.shape[0] // LANES)):
        yield (
            slice(at * LANES, (at + 1) * LANES),
            slice(a * LANES, (a + 1) * LANES),
            slice(b * LANES, (b + 1) * LANES),
        )


def unpack_gram(packed_ref, full_ref):
    count = full_ref.shape[0] // LANES
    rights = right_tiles(count)

    def put(a, b, value):
        full_ref[a * LANES : (a + 1) * LANES, b * LANES : (b + 1) * LANES] = value.astype(BF16)

    for at, (a, b) in enumerate(rights):
        value = packed_ref[at * LANES : (at + 1) * LANES, :]
        put(a, b, value)
        put(b, a, value.astype(F32).T)
    row, column = tile_places()
    at = (len(rights) + (count + 1) // 2) * LANES
    strip = packed_ref[at : at + ID_ROWS, :].astype(F32)
    for pair in range((count + 1) // 2):
        at = (len(rights) + pair) * LANES
        both = packed_ref[at : at + LANES, :].astype(F32)
        turned = both.T
        put(2 * pair, 2 * pair, jnp.where(row <= column, both, turned))
        if 2 * pair + 1 < count:
            second = jnp.where(row > column, both, turned)
            second = jnp.where(row == column, strip[pair : pair + 1, :], second)
            put(2 * pair + 1, 2 * pair + 1, second)


def ffn_kernel(*refs, tok_dev, width, operands, has_gram, has_tiles, for_sibling, gives, scale):
    weight_ref, pieces = refs[0], refs[1 : 1 + operands]
    rest = list(refs[1 + operands :])
    gram_in = rest.pop(0) if has_gram else None
    tiles_in = rest.pop(0) if has_tiles else None
    gram_out, last_out, x_ref, mask_ref, hidden_ref = rest[-5:]
    half, tiles = tok_dev // 2, width // LANES
    expert = lax.axis_index("expert")
    if for_sibling:
        expert = expert + 1 - 2 * (expert % 2)
    expert = expert.astype(F32)
    for b in range(operands // 2):
        hits = None
        for h in range(2):
            piece = pieces[2 * b + h]
            for i in range(half // 16):
                for k in range(tiles):
                    at = (i * tiles + k) * 16
                    row = b * tok_dev + h * half + i * 16
                    x_ref[row : row + 16, k * LANES : (k + 1) * LANES] = piece[at : at + 16, :]
            at = half * tiles
            found = (piece[at : at + ID_ROWS, :tok_dev].astype(F32) == expert).astype(F32)
            hits = found if hits is None else hits + found
        mask_ref[0:1, b * tok_dev : (b + 1) * tok_dev] = jnp.max(hits, axis=0, keepdims=True)
    hidden_width = weight_ref.shape[1] // 2
    step_rows = gram_step(hidden_width)

    gate = product(weight_ref[:, :hidden_width], x_ref[...], TT)
    up = product(weight_ref[:, hidden_width:], x_ref[...], TT)
    hidden_ref[...] = (gate * (0.5 * jnp.tanh(0.5 * gate) + 0.5) * up * mask_ref[0:1, :]).astype(BF16)
    for first in range(0, hidden_width, step_rows):
        rows = slice(first, first + step_rows)
        part = product(hidden_ref[rows, :], hidden_ref[first:, :], NT)
        if has_gram:
            part += gram_in[rows, first:]
        gram_out[rows, first:] = part if tiles_in is not None else part * scale
    if tiles_in is not None:
        for at, rows, columns in tiles_of(gram_out):
            gram_out[rows, columns] = (gram_out[rows, columns] + tiles_in[at, :].astype(F32)) * scale
    if gives == "packed":
        pack_gram(gram_out, last_out)
    elif gives == "tiles":
        for at, rows, columns in tiles_of(gram_out):
            last_out[at, :] = gram_out[rows, columns].astype(BF16)
    else:
        last_out[...] = jnp.zeros_like(last_out)


def ffn(
    weights,
    pieces,
    gram,
    tok_dev,
    tiles=None,
    for_sibling=False,
    gives="tie",
    scale=1.0,
    wait=(),
    hides=False,
):
    hidden_width, width = weights.shape[1] // 2, weights.shape[0]
    count = hidden_width // LANES
    rows = tok_dev * len(pieces) // 2
    last = {
        "tie": kept((8, LANES), F32),
        "tiles": kept((len(upper_tiles(count)) * LANES, LANES), BF16),
        "packed": kept((packed_rows(count), LANES), BF16),
    }[gives]
    more = [array for array in (gram, tiles) if array is not None]
    operands = [weights, *pieces, *more, *wait]
    return pl.pallas_call(
        functools.partial(
            ffn_kernel,
            tok_dev=tok_dev,
            width=width,
            operands=len(pieces),
            has_gram=gram is not None,
            has_tiles=tiles is not None,
            for_sibling=for_sibling,
            gives=gives,
            scale=scale,
        ),
        out_shape=(kept((hidden_width, hidden_width), F32), last),
        in_specs=[VMEM] * len(operands),
        out_specs=(VMEM, VMEM),
        input_output_aliases={} if gram is None else {1 + len(pieces): 0},
        scratch_shapes=[
            pltpu.VMEM((rows, width), BF16),
            pltpu.VMEM((8, rows), F32),
            pltpu.VMEM((hidden_width, rows), BF16),
        ],
        compiler_params=params(8),
        cost_estimate=pl.CostEstimate(
            flops=10**11 if hides else 1000,
            bytes_accessed=1000,
            transcendentals=0,
        ),
    )(*map(here, operands))


def exact(high, low, other_high, other_low):
    total = product(low, other_high, NN)
    total += product(high, other_low, NN)
    return total + product(high, other_high, NN)


def own_kernel(own_ref, high_ref, low_ref, w_hbm, full_ref, panel_ref, w_ref, sem):
    copy = pltpu.make_async_copy(w_hbm, w_ref, sem)
    copy.start()
    count = own_ref.shape[0] // LANES
    for a in range(count):
        for b in range(a, count):
            rows, columns = slice(a * LANES, (a + 1) * LANES), slice(b * LANES, (b + 1) * LANES)
            tile = own_ref[rows, columns]
            full_ref[rows, columns] = tile
            if a != b:
                full_ref[columns, rows] = tile.T
    for first in range(0, own_ref.shape[0], 2 * LANES):
        rows = slice(first, min(first + 2 * LANES, own_ref.shape[0]))
        high, low = split(full_ref[rows, :])
        panel_ref[rows, :] = exact(high, low, high_ref[...], low_ref[...])
    copy.wait()


def own_side(own, high, low, w_down):
    hidden_width, rank = high.shape
    return pl.pallas_call(
        own_kernel,
        out_shape=(
            kept((hidden_width, hidden_width), F32),
            kept((hidden_width, rank), F32),
            kept(w_down.shape, w_down.dtype),
        ),
        in_specs=[VMEM] * 3 + [pl.BlockSpec(memory_space=pl.ANY)],
        out_specs=(VMEM, VMEM, VMEM),
        scratch_shapes=[pltpu.SemaphoreType.DMA],
        compiler_params=params(4),
        cost_estimate=pl.CostEstimate(
            flops=6 * hidden_width * hidden_width * rank,
            bytes_accessed=w_down.size * 2,
            transcendentals=0,
        ),
    )(here(own), here(high), here(low), far(w_down))


def blocks_of(total, most, step, carry=None):
    rows = most if total % most == 0 else total
    return lax.fori_loop(
        0, total // rows, lambda i, c: step(pl.multiple_of(i * rows, rows), rows, c), carry
    )


def power_kernel(*refs, has_other):
    refs = list(refs)
    own_ref, panel_ref = refs[:2]
    other_ref = refs.pop(2) if has_other else None
    first_ref, w_ref, gram_out, power_out = refs[2:6]
    full_ref, other_full, high_ref, image_ref, probe_ref, small_ref, power_ref, sems = refs[6:]
    group = lax.axis_index("group")
    hidden_width, rank = panel_ref.shape
    width = w_ref.shape[0]
    panel = panel_ref[...]
    if has_other:
        unpack_gram(other_ref, other_full)
        panel += product(other_full[...], first_ref[...], NN)
    small_ref[...] = panel.astype(BF16)

    def image_step(first, rows, squares):
        image = product(w_ref[pl.ds(first, rows), :], small_ref[...], NN)
        image_ref[pl.ds(first, rows), :] = image
        return squares + jnp.sum(image * image, axis=0, keepdims=True)

    squares = blocks_of(width, 8 * LANES, image_step, jnp.zeros((1, rank), F32))

    def gram_step(first, rows, carry):
        full = own_ref[pl.ds(first, rows), :]
        if has_other:
            full += other_full[pl.ds(first, rows), :].astype(F32)
        full_ref[pl.ds(first, rows), :] = full
        high_ref[pl.ds(first, rows), :] = full.astype(BF16)
        return carry

    blocks_of(hidden_width, LANES, gram_step)
    panel_rows = gram_out.shape[0]
    gram_copy = pltpu.make_async_copy(
        full_ref.at[pl.ds(pl.multiple_of(group * panel_rows, panel_rows), panel_rows), :],
        gram_out,
        sems.at[0],
    )
    gram_copy.start()
    factor = lax.rsqrt(squares * (1.0 / width) + 1e-06)
    probe_ref[...] = (image_ref[...] * factor).astype(BF16)

    def reduce_step(first, rows, carry):
        reduced = product(w_ref[:, pl.ds(first, rows)], probe_ref[...], TN)
        small_ref[pl.ds(first, rows), :] = reduced.astype(BF16)
        return carry

    blocks_of(hidden_width, 3 * LANES, reduce_step)
    small_ref[...] = product(high_ref[...], small_ref[...], NN).astype(BF16)
    own_rows = power_ref.shape[0]

    def power_copy(first, rows):
        part = pl.ds(first, rows)
        return pltpu.make_async_copy(
            power_ref.at[part, :], power_out.at[part, :], sems.at[1 + first // rows]
        )

    def power_step(first, rows, carry):
        mine = pl.ds(pl.multiple_of(group * own_rows + first, rows), rows)
        power_ref[pl.ds(first, rows), :] = product(w_ref[mine, :], small_ref[...], NN)
        power_copy(first, rows).start()
        return carry

    def power_wait(first, rows, carry):
        power_copy(first, rows).wait()
        return carry

    blocks_of(own_rows, 4 * LANES, power_step)
    gram_copy.wait()
    blocks_of(own_rows, 4 * LANES, power_wait)


def power(own, other, panel, reduced, w_down, group_count):
    width, hidden_width = w_down.shape
    rank = panel.shape[1]
    own_rows = width // group_count
    operands = [own, panel] + ([] if other is None else [other])
    operands += [reduced[0], w_down]
    anywhere = pl.BlockSpec(memory_space=pl.ANY)
    return pl.pallas_call(
        functools.partial(power_kernel, has_other=other is not None),
        out_shape=(
            jax.ShapeDtypeStruct((hidden_width // group_count, hidden_width), F32),
            jax.ShapeDtypeStruct((own_rows, rank), F32),
        ),
        in_specs=[VMEM] * len(operands),
        out_specs=(anywhere, anywhere),
        scratch_shapes=[
            pltpu.VMEM((hidden_width, hidden_width), F32),
            pltpu.VMEM((hidden_width, hidden_width), BF16),
            pltpu.VMEM((hidden_width, hidden_width), BF16),
            pltpu.VMEM((width, rank), F32),
            pltpu.VMEM((width, rank), BF16),
            pltpu.VMEM((hidden_width, rank), BF16),
            pltpu.VMEM((own_rows, rank), F32),
            pltpu.SemaphoreType.DMA((1 + max(1, own_rows // (4 * LANES)),)),
        ],
        compiler_params=params(12),
        cost_estimate=pl.CostEstimate(
            flops=2 * rank * (6 * hidden_width * hidden_width + 3 * width * hidden_width),
            bytes_accessed=w_down.size * 4,
            transcendentals=0,
        ),
    )(*map(here, operands))


def ring_order(chips, across):
    depth = chips // across
    if across < 2 or depth % 2 or depth * across != chips:
        return list(range(chips))
    order = []
    for z in range(depth):
        row = range(1, across) if z % 2 == 0 else range(across - 1, 0, -1)
        order += [z * across + y for y in row]
    return order + [z * across for z in reversed(range(depth))]


def gram_of_all(halves, weights, tok_dev, scale, order, prepare):
    chips = len(order)
    onward = [
        (2 * order[i] + core, 2 * order[(i + 1) % chips] + core)
        for i in range(chips)
        for core in range(2)
    ]
    backward = [(b, a) for a, b in onward]
    sibling = [(i, i ^ 1) for i in range(2 * chips)]

    def send(array, pairs):
        return lax.ppermute(array, "expert", pairs)

    def swap(pieces):
        return [send(piece, sibling) for piece in pieces]

    slots = chips - 1
    sent = {1: (send(halves[0], onward), send(halves[1], backward))}
    weights_s = send(weights, sibling)
    *reduced, first, second = prepare(halves)
    sent[2] = (send(second, onward), send(first, backward))
    tie = reduced[0]
    blocks, mine, others, tiles, pair = [halves], None, None, None, []
    for s in range(1, slots + 1):
        came = [after(tie, array) for array in sent[s]]
        if s + 2 <= slots:
            sent[s + 2] = (send(came[0], onward), send(came[1], backward))
        blocks.append(came if s % 2 else came[::-1])
        if s == slots:
            pieces = swap(blocks[s])
            mine, tie = ffn(weights, [*blocks[s], *blocks[s - 1]], mine, tok_dev, hides=True)
            return *ffn(weights, pieces, mine, tok_dev, tiles, gives="packed", scale=scale), reduced
        if s == slots - 1:
            others, tie = ffn(
                weights_s, blocks[s], others, tok_dev, for_sibling=True, gives="tiles", wait=came
            )
            tiles = send(tie, sibling)
            continue
        if s % 2:
            pair = [*blocks[s - 1], *blocks[s]]
        if s == slots - 2 or s % 2 == 0:
            others, tie = ffn(
                weights_s,
                pair,
                others,
                tok_dev,
                for_sibling=True,
                wait=came,
            )
            if s == slots - 2:
                mine, tie = ffn(weights, pair, mine, tok_dev, wait=[tie])
        else:
            mine, tie = ffn(weights, pair, mine, tok_dev, wait=came)
        if s % 2 == 0:
            pair = []


def on_device(tokens, routes, gate_up, down_weight, sketch):
    owner_count = lax.axis_size("expert")
    group_count = lax.axis_size("group")
    tok_dev = tokens.shape[1]
    order = ring_order(owner_count // 2, group_count)
    scale = 1.0 / (tok_dev * TOPK * group_count)
    halves = pack(tokens[0], routes[0].T)
    w_down = down_weight[0]
    own, packed, reduced = gram_of_all(
        halves,
        gate_up[0],
        tok_dev,
        scale,
        order,
        functools.partial(reduced_first, w_down, sketch[0]),
    )
    if group_count == 2:
        other = lax.ppermute(packed, "group", [(0, 1), (1, 0)])
    else:
        own, other = lax.psum(own, "group"), None
    own, panel, w_down = own_side(own, *reduced, w_down)
    gram, result = power(own, other, panel, reduced, w_down, group_count)
    return gram[None], result[None]


def solution(mesh):
    return jax.shard_map(
        on_device,
        mesh=mesh,
        in_specs=(
            P("group", "expert", None),
            P("group", "expert", None),
            P("expert", None, None),
            P("expert", None, None),
            P("expert", None, None),
        ),
        out_specs=(P("expert", "group", None), P("expert", "group", None)),
        check_vma=False,
    )
```

```python
import functools

import jax
import jax.numpy as jnp
from jax import lax
from jax.experimental import pallas as pl
from jax.experimental.pallas import tpu as pltpu
from jax.sharding import PartitionSpec as P

TOPK = 8
LANES = 128
ID_ROWS = 16
NT = (((1,), (1,)), ((), ()))
NN = (((1,), (0,)), ((), ()))
TN = (((0,), (0,)), ((), ()))
TT = (((0,), (1,)), ((), ()))
BF16 = jnp.bfloat16
F32 = jnp.float32
VMEM = pl.BlockSpec(memory_space=pltpu.VMEM)
MIB = 1 << 20


def here(array):
    return pltpu.with_memory_space_constraint(array, pltpu.VMEM)


def far(array):
    return pltpu.with_memory_space_constraint(array, pltpu.HBM)


def kept(shape, dtype):
    return pltpu.VMEM(tuple(shape), dtype)


def small_cost(hides):
    return pl.CostEstimate(flops=10**11 if hides else 1000, bytes_accessed=1000, transcendentals=0)


def params(mib):
    return pltpu.CompilerParams(vmem_limit_bytes=mib * MIB)


def half_rows(tok_dev, width):
    return tok_dev // 2 * (width // LANES) + ID_ROWS


def pack_kernel(tokens_hbm, routes_hbm, first_ref, second_ref, tokens_ref, routes_ref, sems):
    copies = [
        pltpu.make_async_copy(routes_hbm, routes_ref, sems.at[0]),
        pltpu.make_async_copy(tokens_hbm, tokens_ref, sems.at[1]),
    ]
    for copy in copies:
        copy.start()
    for copy in copies:
        copy.wait()
    tok_dev, width = tokens_ref.shape
    top = routes_ref.shape[0]
    half, tiles = tok_dev // 2, width // LANES
    rows = half_rows(tok_dev, width)
    ids = jnp.concatenate(
        [routes_ref[...].astype(F32), jnp.full((ID_ROWS - top, tok_dev), -1.0, F32)], axis=0
    )
    lane = lax.broadcasted_iota(jnp.int32, ids.shape, 1)
    for h, out_ref in enumerate((first_ref, second_ref)):
        for i in range(half // 16):
            for k in range(tiles):
                at = (i * tiles + k) * 16
                out_ref[at : at + 16, :] = tokens_ref[
                    h * half + i * 16 : h * half + (i + 1) * 16, k * LANES : (k + 1) * LANES
                ]
        mine = (lane >= h * half) & (lane < (h + 1) * half)
        out_ref[rows - ID_ROWS :, :tok_dev] = jnp.where(mine, ids, -1.0).astype(BF16)


def pack(tokens, routes):
    tok_dev, width = tokens.shape
    anywhere = pl.BlockSpec(memory_space=pl.ANY)
    return pl.pallas_call(
        pack_kernel,
        out_shape=(kept((half_rows(tok_dev, width), LANES), BF16),) * 2,
        in_specs=[anywhere, anywhere],
        out_specs=(VMEM, VMEM),
        scratch_shapes=[
            pltpu.VMEM(tokens.shape, tokens.dtype),
            pltpu.VMEM(routes.shape, routes.dtype),
            pltpu.SemaphoreType.DMA((2,)),
        ],
        compiler_params=params(2),
        cost_estimate=pl.CostEstimate(flops=0, bytes_accessed=tokens.size * 4, transcendentals=0),
    )(far(tokens), far(routes))


def split(value):
    high = value.astype(BF16)
    return high, (value - high.astype(F32)).astype(BF16)


def product(left, right, dims):
    return lax.dot_general(left, right, dims, preferred_element_type=F32)


def reduce_kernel(w_hbm, sketch_hbm, *refs):
    *halves, high_ref, low_ref = refs[:4]
    *again, w_ref, sketch_ref, sems = refs[4:]
    copies = [
        pltpu.make_async_copy(w_hbm, w_ref, sems.at[0]),
        pltpu.make_async_copy(sketch_hbm, sketch_ref, sems.at[1]),
    ]
    for copy in copies:
        copy.start()
    for copy in copies:
        copy.wait()
    high_ref[...], low_ref[...] = split(product(w_ref[...], sketch_ref[...], TN))
    for half, copied in zip(halves, again):
        copied[...] = half[...]


def reduced_first(w_down, sketch, halves):
    half = kept((w_down.shape[1], sketch.shape[1]), BF16)
    anywhere = pl.BlockSpec(memory_space=pl.ANY)
    return pl.pallas_call(
        reduce_kernel,
        out_shape=(half, half, *(kept(array.shape, array.dtype) for array in halves)),
        in_specs=[anywhere, anywhere, VMEM, VMEM],
        out_specs=(VMEM,) * 4,
        scratch_shapes=[
            pltpu.VMEM(w_down.shape, w_down.dtype),
            pltpu.VMEM(sketch.shape, sketch.dtype),
            pltpu.SemaphoreType.DMA((2,)),
        ],
        compiler_params=params(6),
        cost_estimate=small_cost(True),
    )(far(w_down), far(sketch), *map(here, halves))


def nothing_kernel(*refs):
    pass


def after(tie, array, *others, hides=False):
    operands = (array, tie, *others)
    return pl.pallas_call(
        nothing_kernel,
        out_shape=kept(array.shape, array.dtype),
        in_specs=[VMEM] * len(operands),
        out_specs=VMEM,
        input_output_aliases={0: 0},
        compiler_params=params(2),
        cost_estimate=small_cost(hides),
    )(*map(here, operands))


def right_tiles(count):
    return [(a, b) for a in range(count) for b in range(a + 1, count)]


def packed_rows(count):
    return (len(right_tiles(count)) + (count + 1) // 2) * LANES + ID_ROWS


def tile_places():
    return (
        lax.broadcasted_iota(jnp.int32, (LANES, LANES), 0),
        lax.broadcasted_iota(jnp.int32, (LANES, LANES), 1),
    )


def gram_step(hidden_width):
    return 2 * LANES if hidden_width % (2 * LANES) == 0 else LANES


def pack_gram(gram_ref, packed_ref):
    count = gram_ref.shape[0] // LANES
    rights = right_tiles(count)

    def tile(a, b):
        return gram_ref[a * LANES : (a + 1) * LANES, b * LANES : (b + 1) * LANES]

    for at, (a, b) in enumerate(rights):
        packed_ref[at * LANES : (at + 1) * LANES, :] = tile(a, b).astype(BF16)
    row, column = tile_places()
    strip = jnp.zeros((ID_ROWS, LANES), F32)
    place = lax.broadcasted_iota(jnp.int32, strip.shape, 0)
    for pair in range((count + 1) // 2):
        at = (len(rights) + pair) * LANES
        both = tile(2 * pair, 2 * pair)
        if 2 * pair + 1 < count:
            second = tile(2 * pair + 1, 2 * pair + 1)
            diagonal = jnp.sum(jnp.where(row == column, second, 0.0), axis=0, keepdims=True)
            strip = jnp.where(place == pair, diagonal, strip)
            both = jnp.where(row <= column, both, second)
        packed_ref[at : at + LANES, :] = both.astype(BF16)
    at = (len(rights) + (count + 1) // 2) * LANES
    packed_ref[at : at + ID_ROWS, :] = strip.astype(BF16)


def upper_tiles(count):
    return [(a, b) for a in range(count) for b in range(a, count)]


def tiles_of(gram_ref):
    for at, (a, b) in enumerate(upper_tiles(gram_ref.shape[0] // LANES)):
        yield (
            slice(at * LANES, (at + 1) * LANES),
            slice(a * LANES, (a + 1) * LANES),
            slice(b * LANES, (b + 1) * LANES),
        )


def unpack_gram(packed_ref, full_ref):
    count = full_ref.shape[0] // LANES
    rights = right_tiles(count)

    def put(a, b, value):
        full_ref[a * LANES : (a + 1) * LANES, b * LANES : (b + 1) * LANES] = value.astype(BF16)

    for at, (a, b) in enumerate(rights):
        value = packed_ref[at * LANES : (at + 1) * LANES, :]
        put(a, b, value)
        put(b, a, value.astype(F32).T)
    row, column = tile_places()
    at = (len(rights) + (count + 1) // 2) * LANES
    strip = packed_ref[at : at + ID_ROWS, :].astype(F32)
    for pair in range((count + 1) // 2):
        at = (len(rights) + pair) * LANES
        both = packed_ref[at : at + LANES, :].astype(F32)
        turned = both.T
        put(2 * pair, 2 * pair, jnp.where(row <= column, both, turned))
        if 2 * pair + 1 < count:
            second = jnp.where(row > column, both, turned)
            second = jnp.where(row == column, strip[pair : pair + 1, :], second)
            put(2 * pair + 1, 2 * pair + 1, second)


def ffn_kernel(*refs, tok_dev, width, operands, has_gram, has_tiles, for_sibling, gives, scale):
    weight_ref, pieces = refs[0], refs[1 : 1 + operands]
    rest = list(refs[1 + operands :])
    gram_in = rest.pop(0) if has_gram else None
    tiles_in = rest.pop(0) if has_tiles else None
    gram_out, last_out, x_ref, mask_ref, hidden_ref = rest[-5:]
    half, tiles = tok_dev // 2, width // LANES
    expert = lax.axis_index("expert")
    if for_sibling:
        expert = expert + 1 - 2 * (expert % 2)
    expert = expert.astype(F32)
    for b in range(operands // 2):
        hits = None
        for h in range(2):
            piece = pieces[2 * b + h]
            for i in range(half // 16):
                for k in range(tiles):
                    at = (i * tiles + k) * 16
                    row = b * tok_dev + h * half + i * 16
                    x_ref[row : row + 16, k * LANES : (k + 1) * LANES] = piece[at : at + 16, :]
            at = half * tiles
            found = (piece[at : at + ID_ROWS, :tok_dev].astype(F32) == expert).astype(F32)
            hits = found if hits is None else hits + found
        mask_ref[0:1, b * tok_dev : (b + 1) * tok_dev] = jnp.max(hits, axis=0, keepdims=True)
    hidden_width = weight_ref.shape[1] // 2
    step_rows = gram_step(hidden_width)

    gate = product(weight_ref[:, :hidden_width], x_ref[...], TT)
    up = product(weight_ref[:, hidden_width:], x_ref[...], TT)
    hidden_ref[...] = (gate * (0.5 * jnp.tanh(0.5 * gate) + 0.5) * up * mask_ref[0:1, :]).astype(BF16)
    for first in range(0, hidden_width, step_rows):
        rows = slice(first, first + step_rows)
        part = product(hidden_ref[rows, :], hidden_ref[first:, :], NT)
        if has_gram:
            part += gram_in[rows, first:]
        gram_out[rows, first:] = part if tiles_in is not None else part * scale
    if tiles_in is not None:
        for at, rows, columns in tiles_of(gram_out):
            gram_out[rows, columns] = (gram_out[rows, columns] + tiles_in[at, :].astype(F32)) * scale
    if gives == "packed":
        pack_gram(gram_out, last_out)
    elif gives == "tiles":
        for at, rows, columns in tiles_of(gram_out):
            last_out[at, :] = gram_out[rows, columns].astype(BF16)
    else:
        last_out[...] = jnp.zeros_like(last_out)


def ffn(
    weights,
    pieces,
    gram,
    tok_dev,
    tiles=None,
    for_sibling=False,
    gives="tie",
    scale=1.0,
    wait=(),
):
    hidden_width, width = weights.shape[1] // 2, weights.shape[0]
    count = hidden_width // LANES
    rows = tok_dev * len(pieces) // 2
    last = {
        "tie": kept((8, LANES), F32),
        "tiles": kept((len(upper_tiles(count)) * LANES, LANES), BF16),
        "packed": kept((packed_rows(count), LANES), BF16),
    }[gives]
    more = [array for array in (gram, tiles) if array is not None]
    operands = [weights, *pieces, *more, *wait]
    return pl.pallas_call(
        functools.partial(
            ffn_kernel,
            tok_dev=tok_dev,
            width=width,
            operands=len(pieces),
            has_gram=gram is not None,
            has_tiles=tiles is not None,
            for_sibling=for_sibling,
            gives=gives,
            scale=scale,
        ),
        out_shape=(kept((hidden_width, hidden_width), F32), last),
        in_specs=[VMEM] * len(operands),
        out_specs=(VMEM, VMEM),
        input_output_aliases={} if gram is None else {1 + len(pieces): 0},
        scratch_shapes=[
            pltpu.VMEM((rows, width), BF16),
            pltpu.VMEM((8, rows), F32),
            pltpu.VMEM((hidden_width, rows), BF16),
        ],
        compiler_params=params(8),
        cost_estimate=small_cost(False),
    )(*map(here, operands))


def exact(high, low, other_high, other_low):
    total = product(low, other_high, NN)
    total += product(high, other_low, NN)
    return total + product(high, other_high, NN)


def own_kernel(own_ref, high_ref, low_ref, w_hbm, full_ref, panel_ref, w_ref, sem):
    copy = pltpu.make_async_copy(w_hbm, w_ref, sem)
    copy.start()
    count = own_ref.shape[0] // LANES
    for a in range(count):
        for b in range(a, count):
            rows, columns = slice(a * LANES, (a + 1) * LANES), slice(b * LANES, (b + 1) * LANES)
            tile = own_ref[rows, columns]
            full_ref[rows, columns] = tile
            if a != b:
                full_ref[columns, rows] = tile.T
    for first in range(0, own_ref.shape[0], 2 * LANES):
        rows = slice(first, min(first + 2 * LANES, own_ref.shape[0]))
        high, low = split(full_ref[rows, :])
        panel_ref[rows, :] = exact(high, low, high_ref[...], low_ref[...])
    copy.wait()


def own_side(own, high, low, w_down):
    hidden_width, rank = high.shape
    return pl.pallas_call(
        own_kernel,
        out_shape=(
            kept((hidden_width, hidden_width), F32),
            kept((hidden_width, rank), F32),
            kept(w_down.shape, w_down.dtype),
        ),
        in_specs=[VMEM] * 3 + [pl.BlockSpec(memory_space=pl.ANY)],
        out_specs=(VMEM, VMEM, VMEM),
        scratch_shapes=[pltpu.SemaphoreType.DMA],
        compiler_params=params(4),
        cost_estimate=pl.CostEstimate(
            flops=6 * hidden_width * hidden_width * rank,
            bytes_accessed=w_down.size * 2,
            transcendentals=0,
        ),
    )(here(own), here(high), here(low), far(w_down))


def blocks_of(total, most, step, carry=None):
    rows = most if total % most == 0 else total
    return lax.fori_loop(
        0, total // rows, lambda i, c: step(pl.multiple_of(i * rows, rows), rows, c), carry
    )


def power_kernel(*refs, has_other):
    refs = list(refs)
    own_ref, panel_ref = refs[:2]
    other_ref = refs.pop(2) if has_other else None
    first_ref, w_ref, gram_out, power_out = refs[2:6]
    full_ref, other_full, high_ref, image_ref, probe_ref, small_ref, power_ref, sems = refs[6:]
    group = lax.axis_index("group")
    hidden_width, rank = panel_ref.shape
    width = w_ref.shape[0]
    panel = panel_ref[...]
    if has_other:
        unpack_gram(other_ref, other_full)
        panel += product(other_full[...], first_ref[...], NN)
    small_ref[...] = panel.astype(BF16)

    def image_step(first, rows, squares):
        image = product(w_ref[pl.ds(first, rows), :], small_ref[...], NN)
        image_ref[pl.ds(first, rows), :] = image
        return squares + jnp.sum(image * image, axis=0, keepdims=True)

    squares = blocks_of(width, 8 * LANES, image_step, jnp.zeros((1, rank), F32))

    def gram_step(first, rows, carry):
        full = own_ref[pl.ds(first, rows), :]
        if has_other:
            full += other_full[pl.ds(first, rows), :].astype(F32)
        full_ref[pl.ds(first, rows), :] = full
        high_ref[pl.ds(first, rows), :] = full.astype(BF16)
        return carry

    blocks_of(hidden_width, LANES, gram_step)
    panel_rows = gram_out.shape[0]
    gram_copy = pltpu.make_async_copy(
        full_ref.at[pl.ds(pl.multiple_of(group * panel_rows, panel_rows), panel_rows), :],
        gram_out,
        sems.at[0],
    )
    gram_copy.start()
    factor = lax.rsqrt(squares * (1.0 / width) + 1e-06)
    probe_ref[...] = (image_ref[...] * factor).astype(BF16)

    def reduce_step(first, rows, carry):
        reduced = product(w_ref[:, pl.ds(first, rows)], probe_ref[...], TN)
        small_ref[pl.ds(first, rows), :] = reduced.astype(BF16)
        return carry

    blocks_of(hidden_width, 3 * LANES, reduce_step)
    small_ref[...] = product(high_ref[...], small_ref[...], NN).astype(BF16)
    own_rows = power_ref.shape[0]

    def power_copy(first, rows):
        part = pl.ds(first, rows)
        return pltpu.make_async_copy(
            power_ref.at[part, :], power_out.at[part, :], sems.at[1 + first // rows]
        )

    def power_step(first, rows, carry):
        mine = pl.ds(pl.multiple_of(group * own_rows + first, rows), rows)
        power_ref[pl.ds(first, rows), :] = product(w_ref[mine, :], small_ref[...], NN)
        power_copy(first, rows).start()
        return carry

    def power_wait(first, rows, carry):
        power_copy(first, rows).wait()
        return carry

    blocks_of(own_rows, 4 * LANES, power_step)
    gram_copy.wait()
    blocks_of(own_rows, 4 * LANES, power_wait)


def power(own, other, panel, reduced, w_down, group_count):
    width, hidden_width = w_down.shape
    rank = panel.shape[1]
    own_rows = width // group_count
    operands = [own, panel] + ([] if other is None else [other])
    operands += [reduced[0], w_down]
    anywhere = pl.BlockSpec(memory_space=pl.ANY)
    return pl.pallas_call(
        functools.partial(power_kernel, has_other=other is not None),
        out_shape=(
            jax.ShapeDtypeStruct((hidden_width // group_count, hidden_width), F32),
            jax.ShapeDtypeStruct((own_rows, rank), F32),
        ),
        in_specs=[VMEM] * len(operands),
        out_specs=(anywhere, anywhere),
        scratch_shapes=[
            pltpu.VMEM((hidden_width, hidden_width), F32),
            pltpu.VMEM((hidden_width, hidden_width), BF16),
            pltpu.VMEM((hidden_width, hidden_width), BF16),
            pltpu.VMEM((width, rank), F32),
            pltpu.VMEM((width, rank), BF16),
            pltpu.VMEM((hidden_width, rank), BF16),
            pltpu.VMEM((own_rows, rank), F32),
            pltpu.SemaphoreType.DMA((1 + max(1, own_rows // (4 * LANES)),)),
        ],
        compiler_params=params(12),
        cost_estimate=pl.CostEstimate(
            flops=2 * rank * (6 * hidden_width * hidden_width + 3 * width * hidden_width),
            bytes_accessed=w_down.size * 4,
            transcendentals=0,
        ),
    )(*map(here, operands))


def ring_order(chips, across):
    depth = chips // across
    if across < 2 or depth % 2 or depth * across != chips:
        return list(range(chips))
    order = []
    for z in range(depth):
        row = range(1, across) if z % 2 == 0 else range(across - 1, 0, -1)
        order += [z * across + y for y in row]
    return order + [z * across for z in reversed(range(depth))]


def gram_of_all(halves, weights, tok_dev, scale, order, prepare):
    chips = len(order)
    onward = [
        (2 * order[i] + core, 2 * order[(i + 1) % chips] + core)
        for i in range(chips)
        for core in range(2)
    ]
    backward = [(b, a) for a, b in onward]
    sibling = [(i, i ^ 1) for i in range(2 * chips)]

    def send(array, pairs):
        return lax.ppermute(array, "expert", pairs)

    def swap(pieces):
        return [send(piece, sibling) for piece in pieces]

    slots = chips - 1
    sent = {1: (send(halves[0], onward), send(halves[1], backward))}
    weights_s = send(weights, sibling)
    *reduced, first, second = prepare(halves)
    sent[2] = (send(second, onward), send(first, backward))
    tie = reduced[0]
    groups = [(i, i + 1) for i in range(slots % 2, slots, 2)]
    groups = [(0,)] * (slots % 2) + groups
    work = {s: [] for s in range(1, slots + 1)}
    for group in groups:
        at = max(group[-1], 1)
        last = group == groups[-1]
        work[at].append((group, last))
        work[at if last or len(group) == 1 else at + 1].append((group, not last))
    blocks, mine, others, tiles = [halves], None, None, None
    for s in range(1, slots + 1):
        came = [after(tie, array) for array in sent[s]]
        if s + 2 <= slots:
            sent[s + 2] = (send(came[0], onward), send(came[1], backward))
        blocks.append(came if s % 2 else came[::-1])
        for group, for_sibling in work[s]:
            pieces = [half for i in group for half in blocks[i]]
            wait = [*came, tie]
            if for_sibling:
                gives = "tiles" if group == groups[-1] else "tie"
                others, tie = ffn(
                    weights_s, pieces, others, tok_dev, for_sibling=True, gives=gives, wait=wait
                )
                if gives == "tiles":
                    tiles = send(tie, sibling)
            else:
                mine, tie = ffn(weights, pieces, mine, tok_dev, wait=wait)
    swapped = swap(blocks[slots])
    tie = after(came[0], tie, came[1], hides=True)
    pieces = [*blocks[slots], *swapped]
    return (
        *ffn(weights, pieces, mine, tok_dev, tiles, gives="packed", scale=scale, wait=[tie]),
        reduced,
    )


def on_device(tokens, routes, gate_up, down_weight, sketch):
    owner_count = lax.axis_size("expert")
    group_count = lax.axis_size("group")
    tok_dev = tokens.shape[1]
    order = ring_order(owner_count // 2, group_count)
    scale = 1.0 / (tok_dev * TOPK * group_count)
    halves = pack(tokens[0], routes[0].T)
    w_down = down_weight[0]
    own, packed, reduced = gram_of_all(
        halves,
        gate_up[0],
        tok_dev,
        scale,
        order,
        functools.partial(reduced_first, w_down, sketch[0]),
    )
    if group_count == 2:
        other = lax.ppermute(packed, "group", [(0, 1), (1, 0)])
    else:
        own, other = lax.psum(own, "group"), None
    own, panel, w_down = own_side(own, *reduced, w_down)
    gram, result = power(own, other, panel, reduced, w_down, group_count)
    return gram[None], result[None]


def solution(mesh):
    return jax.shard_map(
        on_device,
        mesh=mesh,
        in_specs=(
            P("group", "expert", None),
            P("group", "expert", None),
            P("expert", None, None),
            P("expert", None, None),
            P("expert", None, None),
        ),
        out_specs=(P("expert", "group", None), P("expert", "group", None)),
        check_vma=False,
    )
```

```python
import functools

import jax
import jax.numpy as jnp
from jax import lax
from jax.experimental import pallas as pl
from jax.experimental.pallas import tpu as pltpu
from jax.sharding import PartitionSpec as P

TOPK = 8
LANES = 128
ID_ROWS = 16
NT = (((1,), (1,)), ((), ()))
NN = (((1,), (0,)), ((), ()))
TN = (((0,), (0,)), ((), ()))
TT = (((0,), (1,)), ((), ()))
BF16 = jnp.bfloat16
F32 = jnp.float32
VMEM = pl.BlockSpec(memory_space=pltpu.VMEM)
MIB = 1 << 20


def here(array):
    return pltpu.with_memory_space_constraint(array, pltpu.VMEM)


def far(array):
    return pltpu.with_memory_space_constraint(array, pltpu.HBM)


def kept(shape, dtype):
    return pltpu.VMEM(tuple(shape), dtype)


def small_cost(hides):
    return pl.CostEstimate(flops=10**11 if hides else 1000, bytes_accessed=1000, transcendentals=0)


def params(mib):
    return pltpu.CompilerParams(vmem_limit_bytes=mib * MIB)


def half_rows(tok_dev, width):
    return tok_dev // 2 * (width // LANES) + ID_ROWS


def pack_kernel(tokens_hbm, routes_hbm, first_ref, second_ref, tokens_ref, routes_ref, sems):
    copies = [
        pltpu.make_async_copy(routes_hbm, routes_ref, sems.at[0]),
        pltpu.make_async_copy(tokens_hbm, tokens_ref, sems.at[1]),
    ]
    for copy in copies:
        copy.start()
    for copy in copies:
        copy.wait()
    tok_dev, width = tokens_ref.shape
    top = routes_ref.shape[0]
    half, tiles = tok_dev // 2, width // LANES
    rows = half_rows(tok_dev, width)
    ids = jnp.concatenate(
        [routes_ref[...].astype(F32), jnp.full((ID_ROWS - top, tok_dev), -1.0, F32)], axis=0
    )
    lane = lax.broadcasted_iota(jnp.int32, ids.shape, 1)
    for h, out_ref in enumerate((first_ref, second_ref)):
        for i in range(half // 16):
            for k in range(tiles):
                at = (i * tiles + k) * 16
                out_ref[at : at + 16, :] = tokens_ref[
                    h * half + i * 16 : h * half + (i + 1) * 16, k * LANES : (k + 1) * LANES
                ]
        mine = (lane >= h * half) & (lane < (h + 1) * half)
        out_ref[rows - ID_ROWS :, :tok_dev] = jnp.where(mine, ids, -1.0).astype(BF16)


def pack(tokens, routes):
    tok_dev, width = tokens.shape
    anywhere = pl.BlockSpec(memory_space=pl.ANY)
    return pl.pallas_call(
        pack_kernel,
        out_shape=(kept((half_rows(tok_dev, width), LANES), BF16),) * 2,
        in_specs=[anywhere, anywhere],
        out_specs=(VMEM, VMEM),
        scratch_shapes=[
            pltpu.VMEM(tokens.shape, tokens.dtype),
            pltpu.VMEM(routes.shape, routes.dtype),
            pltpu.SemaphoreType.DMA((2,)),
        ],
        compiler_params=params(2),
        cost_estimate=pl.CostEstimate(flops=0, bytes_accessed=tokens.size * 4, transcendentals=0),
    )(far(tokens), far(routes))


def split(value):
    high = value.astype(BF16)
    return high, (value - high.astype(F32)).astype(BF16)


def product(left, right, dims):
    return lax.dot_general(left, right, dims, preferred_element_type=F32)


def reduce_kernel(w_hbm, sketch_hbm, *refs):
    *halves, high_ref, low_ref = refs[:4]
    *again, w_ref, sketch_ref, sems = refs[4:]
    copies = [
        pltpu.make_async_copy(w_hbm, w_ref, sems.at[0]),
        pltpu.make_async_copy(sketch_hbm, sketch_ref, sems.at[1]),
    ]
    for copy in copies:
        copy.start()
    for copy in copies:
        copy.wait()
    high_ref[...], low_ref[...] = split(product(w_ref[...], sketch_ref[...], TN))
    for half, copied in zip(halves, again):
        copied[...] = half[...]


def reduced_first(w_down, sketch, halves):
    half = kept((w_down.shape[1], sketch.shape[1]), BF16)
    anywhere = pl.BlockSpec(memory_space=pl.ANY)
    return pl.pallas_call(
        reduce_kernel,
        out_shape=(half, half, *(kept(array.shape, array.dtype) for array in halves)),
        in_specs=[anywhere, anywhere, VMEM, VMEM],
        out_specs=(VMEM,) * 4,
        scratch_shapes=[
            pltpu.VMEM(w_down.shape, w_down.dtype),
            pltpu.VMEM(sketch.shape, sketch.dtype),
            pltpu.SemaphoreType.DMA((2,)),
        ],
        compiler_params=params(6),
        cost_estimate=small_cost(True),
    )(far(w_down), far(sketch), *map(here, halves))


def nothing_kernel(*refs):
    pass


def after(tie, array, *others, hides=False):
    operands = (array, tie, *others)
    return pl.pallas_call(
        nothing_kernel,
        out_shape=kept(array.shape, array.dtype),
        in_specs=[VMEM] * len(operands),
        out_specs=VMEM,
        input_output_aliases={0: 0},
        compiler_params=params(2),
        cost_estimate=small_cost(hides),
    )(*map(here, operands))


def right_tiles(count):
    return [(a, b) for a in range(count) for b in range(a + 1, count)]


def packed_rows(count):
    return (len(right_tiles(count)) + (count + 1) // 2) * LANES + ID_ROWS


def tile_places():
    return (
        lax.broadcasted_iota(jnp.int32, (LANES, LANES), 0),
        lax.broadcasted_iota(jnp.int32, (LANES, LANES), 1),
    )


def gram_step(hidden_width):
    return 2 * LANES if hidden_width % (2 * LANES) == 0 else LANES


def pack_gram(gram_ref, packed_ref):
    count = gram_ref.shape[0] // LANES
    rights = right_tiles(count)

    def tile(a, b):
        return gram_ref[a * LANES : (a + 1) * LANES, b * LANES : (b + 1) * LANES]

    for at, (a, b) in enumerate(rights):
        packed_ref[at * LANES : (at + 1) * LANES, :] = tile(a, b).astype(BF16)
    row, column = tile_places()
    strip = jnp.zeros((ID_ROWS, LANES), F32)
    place = lax.broadcasted_iota(jnp.int32, strip.shape, 0)
    for pair in range((count + 1) // 2):
        at = (len(rights) + pair) * LANES
        both = tile(2 * pair, 2 * pair)
        if 2 * pair + 1 < count:
            second = tile(2 * pair + 1, 2 * pair + 1)
            diagonal = jnp.sum(jnp.where(row == column, second, 0.0), axis=0, keepdims=True)
            strip = jnp.where(place == pair, diagonal, strip)
            both = jnp.where(row <= column, both, second)
        packed_ref[at : at + LANES, :] = both.astype(BF16)
    at = (len(rights) + (count + 1) // 2) * LANES
    packed_ref[at : at + ID_ROWS, :] = strip.astype(BF16)


def upper_tiles(count):
    return [(a, b) for a in range(count) for b in range(a, count)]


def tiles_of(gram_ref):
    for at, (a, b) in enumerate(upper_tiles(gram_ref.shape[0] // LANES)):
        yield (
            slice(at * LANES, (at + 1) * LANES),
            slice(a * LANES, (a + 1) * LANES),
            slice(b * LANES, (b + 1) * LANES),
        )


def unpack_gram(packed_ref, full_ref):
    count = full_ref.shape[0] // LANES
    rights = right_tiles(count)

    def put(a, b, value):
        full_ref[a * LANES : (a + 1) * LANES, b * LANES : (b + 1) * LANES] = value.astype(BF16)

    for at, (a, b) in enumerate(rights):
        value = packed_ref[at * LANES : (at + 1) * LANES, :]
        put(a, b, value)
        put(b, a, value.astype(F32).T)
    row, column = tile_places()
    at = (len(rights) + (count + 1) // 2) * LANES
    strip = packed_ref[at : at + ID_ROWS, :].astype(F32)
    for pair in range((count + 1) // 2):
        at = (len(rights) + pair) * LANES
        both = packed_ref[at : at + LANES, :].astype(F32)
        turned = both.T
        put(2 * pair, 2 * pair, jnp.where(row <= column, both, turned))
        if 2 * pair + 1 < count:
            second = jnp.where(row > column, both, turned)
            second = jnp.where(row == column, strip[pair : pair + 1, :], second)
            put(2 * pair + 1, 2 * pair + 1, second)


def ffn_kernel(*refs, tok_dev, width, operands, has_gram, has_tiles, for_sibling, gives, scale):
    weight_ref, pieces = refs[0], refs[1 : 1 + operands]
    rest = list(refs[1 + operands :])
    gram_in = rest.pop(0) if has_gram else None
    tiles_in = rest.pop(0) if has_tiles else None
    gram_out, last_out, x_ref, mask_ref, hidden_ref = rest[-5:]
    half, tiles = tok_dev // 2, width // LANES
    expert = lax.axis_index("expert")
    if for_sibling:
        expert = expert + 1 - 2 * (expert % 2)
    expert = expert.astype(F32)
    for b in range(operands // 2):
        hits = None
        for h in range(2):
            piece = pieces[2 * b + h]
            for i in range(half // 16):
                for k in range(tiles):
                    at = (i * tiles + k) * 16
                    row = b * tok_dev + h * half + i * 16
                    x_ref[row : row + 16, k * LANES : (k + 1) * LANES] = piece[at : at + 16, :]
            at = half * tiles
            found = (piece[at : at + ID_ROWS, :tok_dev].astype(F32) == expert).astype(F32)
            hits = found if hits is None else hits + found
        mask_ref[0:1, b * tok_dev : (b + 1) * tok_dev] = jnp.max(hits, axis=0, keepdims=True)
    hidden_width = weight_ref.shape[1] // 2
    step_rows = gram_step(hidden_width)

    gate = product(weight_ref[:, :hidden_width], x_ref[...], TT)
    up = product(weight_ref[:, hidden_width:], x_ref[...], TT)
    hidden_ref[...] = (gate * (0.5 * jnp.tanh(0.5 * gate) + 0.5) * up * mask_ref[0:1, :]).astype(BF16)
    for first in range(0, hidden_width, step_rows):
        rows = slice(first, first + step_rows)
        part = product(hidden_ref[rows, :], hidden_ref[first:, :], NT)
        if has_gram:
            part += gram_in[rows, first:]
        gram_out[rows, first:] = part if tiles_in is not None else part * scale
    if tiles_in is not None:
        for at, rows, columns in tiles_of(gram_out):
            gram_out[rows, columns] = (gram_out[rows, columns] + tiles_in[at, :].astype(F32)) * scale
    if gives == "packed":
        pack_gram(gram_out, last_out)
    elif gives == "tiles":
        for at, rows, columns in tiles_of(gram_out):
            last_out[at, :] = gram_out[rows, columns].astype(BF16)
    else:
        last_out[...] = jnp.zeros_like(last_out)


def ffn(
    weights,
    pieces,
    gram,
    tok_dev,
    tiles=None,
    for_sibling=False,
    gives="tie",
    scale=1.0,
    wait=(),
):
    hidden_width, width = weights.shape[1] // 2, weights.shape[0]
    count = hidden_width // LANES
    rows = tok_dev * len(pieces) // 2
    last = {
        "tie": kept((8, LANES), F32),
        "tiles": kept((len(upper_tiles(count)) * LANES, LANES), BF16),
        "packed": kept((packed_rows(count), LANES), BF16),
    }[gives]
    more = [array for array in (gram, tiles) if array is not None]
    operands = [weights, *pieces, *more, *wait]
    return pl.pallas_call(
        functools.partial(
            ffn_kernel,
            tok_dev=tok_dev,
            width=width,
            operands=len(pieces),
            has_gram=gram is not None,
            has_tiles=tiles is not None,
            for_sibling=for_sibling,
            gives=gives,
            scale=scale,
        ),
        out_shape=(kept((hidden_width, hidden_width), F32), last),
        in_specs=[VMEM] * len(operands),
        out_specs=(VMEM, VMEM),
        input_output_aliases={} if gram is None else {1 + len(pieces): 0},
        scratch_shapes=[
            pltpu.VMEM((rows, width), BF16),
            pltpu.VMEM((8, rows), F32),
            pltpu.VMEM((hidden_width, rows), BF16),
        ],
        compiler_params=params(8),
        cost_estimate=small_cost(False),
    )(*map(here, operands))


def exact(high, low, other_high, other_low):
    total = product(low, other_high, NN)
    total += product(high, other_low, NN)
    return total + product(high, other_high, NN)


def own_kernel(own_ref, high_ref, low_ref, w_hbm, full_ref, panel_ref, w_ref, square_ref, sem):
    copy = pltpu.make_async_copy(w_hbm, w_ref, sem)
    copy.start()
    for _, rows, columns in tiles_of(own_ref):
        tile = own_ref[rows, columns]
        full_ref[rows, columns] = tile
        if rows != columns:
            full_ref[columns, rows] = tile.T
    hidden_width = own_ref.shape[0]
    step_rows = gram_step(hidden_width)
    for first in range(0, hidden_width, step_rows):
        rows = slice(first, first + step_rows)
        high, low = split(full_ref[rows, :])
        panel_ref[rows, :] = exact(high, low, high_ref[...], low_ref[...])
    copy.wait()
    for first in range(0, hidden_width, step_rows):
        rows = slice(first, first + step_rows)
        square_ref[rows, :] = product(w_ref[:, rows], w_ref[...], TN).astype(BF16)


def own_side(own, high, low, w_down):
    hidden_width, rank = high.shape
    return pl.pallas_call(
        own_kernel,
        out_shape=(
            kept((hidden_width, hidden_width), F32),
            kept((hidden_width, rank), F32),
            kept(w_down.shape, w_down.dtype),
            kept((hidden_width, hidden_width), BF16),
        ),
        in_specs=[VMEM] * 3 + [pl.BlockSpec(memory_space=pl.ANY)],
        out_specs=(VMEM,) * 4,
        scratch_shapes=[pltpu.SemaphoreType.DMA],
        compiler_params=params(6),
        cost_estimate=small_cost(False),
    )(here(own), here(high), here(low), far(w_down))


def blocks_of(total, most, step, carry=None):
    rows = most if total % most == 0 else total
    return lax.fori_loop(
        0, total // rows, lambda i, c: step(pl.multiple_of(i * rows, rows), rows, c), carry
    )


def power_kernel(*refs, has_other):
    refs = list(refs)
    own_ref, panel_ref = refs[:2]
    other_ref = refs.pop(2) if has_other else None
    first_ref, w_ref, square_ref, gram_out, power_out = refs[2:7]
    full_ref, other_full, high_ref, small_ref, power_ref, sems = refs[7:]
    group = lax.axis_index("group")
    hidden_width, rank = panel_ref.shape
    width = w_ref.shape[0]
    panel = panel_ref[...]
    if has_other:
        unpack_gram(other_ref, other_full)
        panel += product(other_full[...], first_ref[...], NN)
    small_ref[...] = panel.astype(BF16)

    for first in range(0, hidden_width, LANES):
        rows = slice(first, first + LANES)
        full = own_ref[rows, :]
        if has_other:
            full += other_full[rows, :].astype(F32)
        full_ref[rows, :] = full
        high_ref[rows, :] = full.astype(BF16)
    panel_rows = gram_out.shape[0]
    gram_copy = pltpu.make_async_copy(
        full_ref.at[pl.ds(pl.multiple_of(group * panel_rows, panel_rows), panel_rows), :],
        gram_out,
        sems.at[0],
    )
    gram_copy.start()
    panel = small_ref[...]
    reduced = product(square_ref[...], panel, NN)
    squares = jnp.sum(panel.astype(F32) * reduced, axis=0, keepdims=True)
    factor = lax.rsqrt(jnp.maximum(squares, 0.0) * (1.0 / width) + 1e-06)
    small_ref[...] = (reduced * factor).astype(BF16)
    small_ref[...] = product(high_ref[...], small_ref[...], NN).astype(BF16)
    own_rows = power_ref.shape[0]

    def power_copy(first, rows):
        part = pl.ds(first, rows)
        return pltpu.make_async_copy(
            power_ref.at[part, :], power_out.at[part, :], sems.at[1 + first // rows]
        )

    def power_step(first, rows, carry):
        mine = pl.ds(pl.multiple_of(group * own_rows + first, rows), rows)
        power_ref[pl.ds(first, rows), :] = product(w_ref[mine, :], small_ref[...], NN)
        power_copy(first, rows).start()
        return carry

    def power_wait(first, rows, carry):
        power_copy(first, rows).wait()
        return carry

    blocks_of(own_rows, 4 * LANES, power_step)
    gram_copy.wait()
    blocks_of(own_rows, 4 * LANES, power_wait)


def power(own, other, panel, reduced, w_down, square, group_count):
    width, hidden_width = w_down.shape
    rank = panel.shape[1]
    own_rows = width // group_count
    operands = [own, panel] + ([] if other is None else [other])
    operands += [reduced[0], w_down, square]
    anywhere = pl.BlockSpec(memory_space=pl.ANY)
    return pl.pallas_call(
        functools.partial(power_kernel, has_other=other is not None),
        out_shape=(
            jax.ShapeDtypeStruct((hidden_width // group_count, hidden_width), F32),
            jax.ShapeDtypeStruct((own_rows, rank), F32),
        ),
        in_specs=[VMEM] * len(operands),
        out_specs=(anywhere, anywhere),
        scratch_shapes=[
            pltpu.VMEM((hidden_width, hidden_width), F32),
            pltpu.VMEM((hidden_width, hidden_width), BF16),
            pltpu.VMEM((hidden_width, hidden_width), BF16),
            pltpu.VMEM((hidden_width, rank), BF16),
            pltpu.VMEM((own_rows, rank), F32),
            pltpu.SemaphoreType.DMA((1 + max(1, own_rows // (4 * LANES)),)),
        ],
        compiler_params=params(12),
        cost_estimate=pl.CostEstimate(
            flops=2 * rank * (6 * hidden_width * hidden_width + 3 * width * hidden_width),
            bytes_accessed=w_down.size * 4,
            transcendentals=0,
        ),
    )(*map(here, operands))


def ring_order(chips, across):
    depth = chips // across
    if across < 2 or depth % 2 or depth * across != chips:
        return list(range(chips))
    order = []
    for z in range(depth):
        row = range(1, across) if z % 2 == 0 else range(across - 1, 0, -1)
        order += [z * across + y for y in row]
    return order + [z * across for z in reversed(range(depth))]


def gram_of_all(halves, weights, tok_dev, scale, order, prepare):
    chips = len(order)
    onward = [
        (2 * order[i] + core, 2 * order[(i + 1) % chips] + core)
        for i in range(chips)
        for core in range(2)
    ]
    backward = [(b, a) for a, b in onward]
    sibling = [(i, i ^ 1) for i in range(2 * chips)]

    def send(array, pairs):
        return lax.ppermute(array, "expert", pairs)

    def swap(pieces):
        return [send(piece, sibling) for piece in pieces]

    slots = chips - 1
    sent = {1: (send(halves[0], onward), send(halves[1], backward))}
    weights_s = send(weights, sibling)
    *reduced, first, second = prepare(halves)
    sent[2] = (send(second, onward), send(first, backward))
    tie = reduced[0]
    groups = [(i, i + 1) for i in range(slots % 2, slots, 2)]
    groups = [(0,)] * (slots % 2) + groups
    work = {s: [] for s in range(1, slots + 1)}
    for group in groups:
        at = max(group[-1], 1)
        last = group == groups[-1]
        work[at].append((group, last))
        work[at if last or len(group) == 1 else at + 1].append((group, not last))
    blocks, mine, others, tiles = [halves], None, None, None
    for s in range(1, slots + 1):
        came = [after(tie, array) for array in sent[s]]
        if s + 2 <= slots:
            sent[s + 2] = (send(came[0], onward), send(came[1], backward))
        blocks.append(came if s % 2 else came[::-1])
        for group, for_sibling in work[s]:
            pieces = [half for i in group for half in blocks[i]]
            wait = [*came, tie]
            if for_sibling:
                gives = "tiles" if group == groups[-1] else "tie"
                others, tie = ffn(
                    weights_s, pieces, others, tok_dev, for_sibling=True, gives=gives, wait=wait
                )
                if gives == "tiles":
                    tiles = send(tie, sibling)
            else:
                mine, tie = ffn(weights, pieces, mine, tok_dev, wait=wait)
    swapped = swap(blocks[slots])
    tie = after(came[0], tie, came[1], hides=True)
    pieces = [*blocks[slots], *swapped]
    return (
        *ffn(weights, pieces, mine, tok_dev, tiles, gives="packed", scale=scale, wait=[tie]),
        reduced,
    )


def on_device(tokens, routes, gate_up, down_weight, sketch):
    owner_count = lax.axis_size("expert")
    group_count = lax.axis_size("group")
    tok_dev = tokens.shape[1]
    order = ring_order(owner_count // 2, group_count)
    scale = 1.0 / (tok_dev * TOPK * group_count)
    halves = pack(tokens[0], routes[0].T)
    w_down = down_weight[0]
    own, packed, reduced = gram_of_all(
        halves,
        gate_up[0],
        tok_dev,
        scale,
        order,
        functools.partial(reduced_first, w_down, sketch[0]),
    )
    if group_count == 2:
        other = lax.ppermute(packed, "group", [(0, 1), (1, 0)])
    else:
        own, other = lax.psum(own, "group"), None
    own, panel, w_down, square = own_side(own, *reduced, w_down)
    gram, result = power(own, other, panel, reduced, w_down, square, group_count)
    return gram[None], result[None]


def solution(mesh):
    return jax.shard_map(
        on_device,
        mesh=mesh,
        in_specs=(
            P("group", "expert", None),
            P("group", "expert", None),
            P("expert", None, None),
            P("expert", None, None),
            P("expert", None, None),
        ),
        out_specs=(P("expert", "group", None), P("expert", "group", None)),
        check_vma=False,
    )
```

```python
import functools

import jax
import jax.numpy as jnp
from jax import lax
from jax.experimental import pallas as pl
from jax.experimental.pallas import tpu as pltpu
from jax.sharding import PartitionSpec as P

TOPK = 8
LANES = 128
FRONT = 2
ID_ROWS = 16
NT = (((1,), (1,)), ((), ()))
NN = (((1,), (0,)), ((), ()))
TN = (((0,), (0,)), ((), ()))
TT = (((0,), (1,)), ((), ()))
BF16 = jnp.bfloat16
F32 = jnp.float32
VMEM = pl.BlockSpec(memory_space=pltpu.VMEM)
MIB = 1 << 20


def here(array):
    return pltpu.with_memory_space_constraint(array, pltpu.VMEM)


def far(array):
    return pltpu.with_memory_space_constraint(array, pltpu.HBM)


def kept(shape, dtype):
    return pltpu.VMEM(tuple(shape), dtype)


def small_cost(hides):
    return pl.CostEstimate(flops=10**11 if hides else 1000, bytes_accessed=1000, transcendentals=0)


def params(mib):
    return pltpu.CompilerParams(vmem_limit_bytes=mib * MIB)


def half_rows(tok_dev, width):
    return tok_dev // 2 * (width // LANES) + ID_ROWS


def pack_kernel(tokens_hbm, routes_hbm, first_ref, second_ref, tokens_ref, routes_ref, sems):
    copies = [
        pltpu.make_async_copy(routes_hbm, routes_ref, sems.at[0]),
        pltpu.make_async_copy(tokens_hbm, tokens_ref, sems.at[1]),
    ]
    for copy in copies:
        copy.start()
    for copy in copies:
        copy.wait()
    tok_dev, width = tokens_ref.shape
    top = routes_ref.shape[0]
    half, tiles = tok_dev // 2, width // LANES
    rows = half_rows(tok_dev, width)
    ids = jnp.concatenate(
        [routes_ref[...].astype(F32), jnp.full((ID_ROWS - top, tok_dev), -1.0, F32)], axis=0
    )
    lane = lax.broadcasted_iota(jnp.int32, ids.shape, 1)
    for h, out_ref in enumerate((first_ref, second_ref)):
        for i in range(half // 16):
            for k in range(tiles):
                at = (i * tiles + k) * 16
                out_ref[at : at + 16, :] = tokens_ref[
                    h * half + i * 16 : h * half + (i + 1) * 16, k * LANES : (k + 1) * LANES
                ]
        mine = (lane >= h * half) & (lane < (h + 1) * half)
        out_ref[rows - ID_ROWS :, :tok_dev] = jnp.where(mine, ids, -1.0).astype(BF16)


def pack(tokens, routes):
    tok_dev, width = tokens.shape
    anywhere = pl.BlockSpec(memory_space=pl.ANY)
    return pl.pallas_call(
        pack_kernel,
        out_shape=(kept((half_rows(tok_dev, width), LANES), BF16),) * 2,
        in_specs=[anywhere, anywhere],
        out_specs=(VMEM, VMEM),
        scratch_shapes=[
            pltpu.VMEM(tokens.shape, tokens.dtype),
            pltpu.VMEM(routes.shape, routes.dtype),
            pltpu.SemaphoreType.DMA((2,)),
        ],
        compiler_params=params(2),
        cost_estimate=pl.CostEstimate(flops=0, bytes_accessed=tokens.size * 4, transcendentals=0),
    )(far(tokens), far(routes))


def split(value):
    high = value.astype(BF16)
    return high, (value - high.astype(F32)).astype(BF16)


def product(left, right, dims):
    return lax.dot_general(left, right, dims, preferred_element_type=F32)


def reduce_kernel(w_hbm, sketch_hbm, *refs):
    *halves, high_ref, low_ref = refs[:4]
    *again, w_ref, sketch_ref, sems = refs[4:]
    copies = [
        pltpu.make_async_copy(w_hbm, w_ref, sems.at[0]),
        pltpu.make_async_copy(sketch_hbm, sketch_ref, sems.at[1]),
    ]
    for copy in copies:
        copy.start()
    for copy in copies:
        copy.wait()
    high_ref[...], low_ref[...] = split(product(w_ref[...], sketch_ref[...], TN))
    for half, copied in zip(halves, again):
        copied[...] = half[...]


def reduced_first(w_down, sketch, halves):
    half = kept((w_down.shape[1], sketch.shape[1]), BF16)
    anywhere = pl.BlockSpec(memory_space=pl.ANY)
    return pl.pallas_call(
        reduce_kernel,
        out_shape=(half, half, *(kept(array.shape, array.dtype) for array in halves)),
        in_specs=[anywhere, anywhere, VMEM, VMEM],
        out_specs=(VMEM,) * 4,
        scratch_shapes=[
            pltpu.VMEM(w_down.shape, w_down.dtype),
            pltpu.VMEM(sketch.shape, sketch.dtype),
            pltpu.SemaphoreType.DMA((2,)),
        ],
        compiler_params=params(6),
        cost_estimate=small_cost(True),
    )(far(w_down), far(sketch), *map(here, halves))


def nothing_kernel(*refs):
    pass


def after(tie, array, *others, hides=False):
    operands = (array, tie, *others)
    return pl.pallas_call(
        nothing_kernel,
        out_shape=kept(array.shape, array.dtype),
        in_specs=[VMEM] * len(operands),
        out_specs=VMEM,
        input_output_aliases={0: 0},
        compiler_params=params(2),
        cost_estimate=small_cost(hides),
    )(*map(here, operands))


def right_tiles(count, part):
    rows = range(count)[:FRONT] if part == 0 else range(count)[FRONT:]
    return [(a, b) for a in rows for b in range(a + 1, count)]


def pairs_of(count, part):
    return range(0, min(count, FRONT), 2) if part == 0 else range(FRONT, count, 2)


def packed_rows(count, part):
    return (len(right_tiles(count, part)) + len(pairs_of(count, part))) * LANES + ID_ROWS


def tile_places():
    return (
        lax.broadcasted_iota(jnp.int32, (LANES, LANES), 0),
        lax.broadcasted_iota(jnp.int32, (LANES, LANES), 1),
    )


def gram_step(hidden_width):
    return 2 * LANES if hidden_width % (2 * LANES) == 0 else LANES


def pack_gram(gram_ref, packed_ref, part):
    count = gram_ref.shape[0] // LANES
    rights = right_tiles(count, part)

    def tile(a, b):
        return gram_ref[a * LANES : (a + 1) * LANES, b * LANES : (b + 1) * LANES]

    for at, (a, b) in enumerate(rights):
        packed_ref[at * LANES : (at + 1) * LANES, :] = tile(a, b).astype(BF16)
    row, column = tile_places()
    strip = jnp.zeros((ID_ROWS, LANES), F32)
    place = lax.broadcasted_iota(jnp.int32, strip.shape, 0)
    at = len(rights) * LANES
    for i, first in enumerate(pairs_of(count, part)):
        both = tile(first, first)
        if first + 1 < count:
            second = tile(first + 1, first + 1)
            diagonal = jnp.sum(jnp.where(row == column, second, 0.0), axis=0, keepdims=True)
            strip = jnp.where(place == i, diagonal, strip)
            both = jnp.where(row <= column, both, second)
        packed_ref[at : at + LANES, :] = both.astype(BF16)
        at += LANES
    packed_ref[at : at + ID_ROWS, :] = strip.astype(BF16)


def upper_tiles(count):
    return [(a, b) for a in range(count) for b in range(a, count)]


def tiles_of(gram_ref):
    for at, (a, b) in enumerate(upper_tiles(gram_ref.shape[0] // LANES)):
        yield (
            slice(at * LANES, (at + 1) * LANES),
            slice(a * LANES, (a + 1) * LANES),
            slice(b * LANES, (b + 1) * LANES),
        )


def unpack_gram(packed_ref, full_ref, part):
    count = full_ref.shape[0] // LANES
    rights = right_tiles(count, part)

    def put(a, b, value):
        full_ref[a * LANES : (a + 1) * LANES, b * LANES : (b + 1) * LANES] = value.astype(BF16)

    for at, (a, b) in enumerate(rights):
        value = packed_ref[at * LANES : (at + 1) * LANES, :]
        put(a, b, value)
        put(b, a, value.astype(F32).T)
    row, column = tile_places()
    pairs = pairs_of(count, part)
    at = (len(rights) + len(pairs)) * LANES
    strip = packed_ref[at : at + ID_ROWS, :].astype(F32)
    for i, first in enumerate(pairs):
        at = (len(rights) + i) * LANES
        both = packed_ref[at : at + LANES, :].astype(F32)
        turned = both.T
        put(first, first, jnp.where(row <= column, both, turned))
        if first + 1 < count:
            second = jnp.where(row > column, both, turned)
            second = jnp.where(row == column, strip[i : i + 1, :], second)
            put(first + 1, first + 1, second)


def ffn_kernel(*refs, tok_dev, width, operands, has_gram, for_sibling, gives, scale):
    weight_ref, pieces = refs[0], refs[1 : 1 + operands]
    rest = list(refs[1 + operands :])
    gram_in = rest.pop(0) if has_gram else None
    gram_out, last_out, hidden_ref, x_ref, mask_ref = rest[-5:]
    half, tiles = tok_dev // 2, width // LANES
    expert = lax.axis_index("expert")
    if for_sibling:
        expert = expert + 1 - 2 * (expert % 2)
    expert = expert.astype(F32)
    for b in range(operands // 2):
        hits = None
        for h in range(2):
            piece = pieces[2 * b + h]
            for i in range(half // 16):
                for k in range(tiles):
                    at = (i * tiles + k) * 16
                    row = b * tok_dev + h * half + i * 16
                    x_ref[row : row + 16, k * LANES : (k + 1) * LANES] = piece[at : at + 16, :]
            at = half * tiles
            found = (piece[at : at + ID_ROWS, :tok_dev].astype(F32) == expert).astype(F32)
            hits = found if hits is None else hits + found
        mask_ref[0:1, b * tok_dev : (b + 1) * tok_dev] = jnp.max(hits, axis=0, keepdims=True)
    hidden_width = weight_ref.shape[1] // 2
    step_rows = gram_step(hidden_width)

    gate = product(weight_ref[:, :hidden_width], x_ref[...], TT)
    up = product(weight_ref[:, hidden_width:], x_ref[...], TT)
    hidden_ref[...] = (gate * (0.5 * jnp.tanh(0.5 * gate) + 0.5) * up * mask_ref[0:1, :]).astype(BF16)
    for first in range(0, FRONT * LANES if gives == "front" else hidden_width, step_rows):
        gram_rows(hidden_ref, gram_in, gram_out, first, step_rows, scale)
    if gives == "front":
        pack_gram(gram_out, last_out, 0)
    elif gives == "tiles":
        for at, rows, columns in tiles_of(gram_out):
            last_out[at, :] = gram_out[rows, columns].astype(BF16)
    else:
        last_out[...] = jnp.zeros_like(last_out)


def gram_rows(hidden_ref, gram_in, gram_out, first, count, scale):
    rows = slice(first, first + count)
    part = product(hidden_ref[rows, :], hidden_ref[first:, :], NT)
    if gram_in is not None:
        part += gram_in[rows, first:]
    gram_out[rows, first:] = part * scale


def rest_kernel(gram_in, hidden_ref, gram_out, packed_out, *, scale):
    hidden_width = gram_in.shape[0]
    step_rows = gram_step(hidden_width)
    for first in range(FRONT * LANES, hidden_width, step_rows):
        gram_rows(hidden_ref, gram_in, gram_out, first, step_rows, scale)
    pack_gram(gram_out, packed_out, 1)


def rest_of(gram, hidden, scale):
    count = gram.shape[0] // LANES
    return pl.pallas_call(
        functools.partial(rest_kernel, scale=scale),
        out_shape=(kept(gram.shape, gram.dtype), kept((packed_rows(count, 1), LANES), BF16)),
        in_specs=[VMEM, VMEM],
        out_specs=(VMEM, VMEM),
        input_output_aliases={0: 0},
        compiler_params=params(10),
        cost_estimate=small_cost(False),
    )(here(gram), here(hidden))


def ffn(
    weights,
    pieces,
    gram,
    tok_dev,
    for_sibling=False,
    gives="tie",
    scale=1.0,
    wait=(),
):
    hidden_width, width = weights.shape[1] // 2, weights.shape[0]
    count = hidden_width // LANES
    rows = tok_dev * len(pieces) // 2
    last = {
        "tie": kept((8, LANES), F32),
        "tiles": kept((len(upper_tiles(count)) * LANES, LANES), BF16),
        "front": kept((packed_rows(count, 0), LANES), BF16),
    }[gives]
    hidden = pltpu.VMEM((hidden_width, rows), BF16)
    front = gives == "front"
    operands = [weights, *pieces, *([] if gram is None else [gram]), *wait]
    return pl.pallas_call(
        functools.partial(
            ffn_kernel,
            tok_dev=tok_dev,
            width=width,
            operands=len(pieces),
            has_gram=gram is not None,
            for_sibling=for_sibling,
            gives=gives,
            scale=scale,
        ),
        out_shape=(kept((hidden_width, hidden_width), F32), last, *([hidden] * front)),
        in_specs=[VMEM] * len(operands),
        out_specs=(VMEM,) * (2 + front),
        input_output_aliases={} if gram is None else {1 + len(pieces): 0},
        scratch_shapes=[
            *([hidden] * (not front)),
            pltpu.VMEM((rows, width), BF16),
            pltpu.VMEM((8, rows), F32),
        ],
        compiler_params=params(8),
        cost_estimate=small_cost(False),
    )(*map(here, operands))


def merge_kernel(gram_ref, tiles_ref, tie_ref, out_ref):
    for at, rows, columns in tiles_of(gram_ref):
        out_ref[rows, columns] = gram_ref[rows, columns] + tiles_ref[at, :].astype(F32)


def merged(gram, tiles, tie):
    return pl.pallas_call(
        merge_kernel,
        out_shape=kept(gram.shape, gram.dtype),
        in_specs=[VMEM] * 3,
        out_specs=VMEM,
        input_output_aliases={0: 0},
        compiler_params=params(10),
        cost_estimate=small_cost(False),
    )(here(gram), here(tiles), here(tie))


def exact(high, low, other_high, other_low):
    total = product(low, other_high, NN)
    total += product(high, other_low, NN)
    return total + product(high, other_high, NN)


def own_kernel(own_ref, high_ref, low_ref, w_hbm, full_ref, panel_ref, w_ref, square_ref, sem):
    copy = pltpu.make_async_copy(w_hbm, w_ref, sem)
    copy.start()
    for _, rows, columns in tiles_of(own_ref):
        tile = own_ref[rows, columns]
        full_ref[rows, columns] = tile
        if rows != columns:
            full_ref[columns, rows] = tile.T
    hidden_width = own_ref.shape[0]
    step_rows = gram_step(hidden_width)
    for first in range(0, hidden_width, step_rows):
        rows = slice(first, first + step_rows)
        high, low = split(full_ref[rows, :])
        panel_ref[rows, :] = exact(high, low, high_ref[...], low_ref[...])
    copy.wait()
    for first in range(0, hidden_width, step_rows):
        rows = slice(first, first + step_rows)
        square_ref[rows, :] = product(w_ref[:, rows], w_ref[...], TN).astype(BF16)


def own_side(own, high, low, w_down):
    hidden_width, rank = high.shape
    return pl.pallas_call(
        own_kernel,
        out_shape=(
            kept((hidden_width, hidden_width), F32),
            kept((hidden_width, rank), F32),
            kept(w_down.shape, w_down.dtype),
            kept((hidden_width, hidden_width), BF16),
        ),
        in_specs=[VMEM] * 3 + [pl.BlockSpec(memory_space=pl.ANY)],
        out_specs=(VMEM,) * 4,
        scratch_shapes=[pltpu.SemaphoreType.DMA],
        compiler_params=params(6),
        cost_estimate=small_cost(False),
    )(here(own), here(high), here(low), far(w_down))


def blocks_of(total, most, step, carry=None):
    rows = most if total % most == 0 else total
    return lax.fori_loop(
        0, total // rows, lambda i, c: step(pl.multiple_of(i * rows, rows), rows, c), carry
    )


def front_kernel(own_in, panel_in, front_ref, first_ref, own_out, panel_out, other_ref):
    rows = slice(0, FRONT * LANES)
    other_ref[FRONT * LANES :, FRONT * LANES :] = jnp.zeros_like(
        other_ref[FRONT * LANES :, FRONT * LANES :]
    )
    unpack_gram(front_ref, other_ref, 0)
    panel_out[...] = panel_in[...] + product(other_ref[...], first_ref[...], NN)
    own_out[rows, :] = own_in[rows, :] + other_ref[rows, :].astype(F32)


def with_front(own, panel, front, first):
    return pl.pallas_call(
        front_kernel,
        out_shape=(
            kept(own.shape, F32),
            kept(panel.shape, F32),
            kept(own.shape, BF16),
        ),
        in_specs=[VMEM] * 4,
        out_specs=(VMEM,) * 3,
        input_output_aliases={0: 0, 1: 1},
        compiler_params=params(10),
        cost_estimate=small_cost(False),
    )(*map(here, (own, panel, front, first)))


def power_kernel(*refs, has_other):
    refs = list(refs)
    own_ref, panel_ref = refs[:2]
    front_ref, rest_ref = [refs.pop(2) for _ in range(2)] if has_other else (None, None)
    first_ref, w_ref, square_ref, gram_out, power_out = refs[2:7]
    full_ref, other_full, high_ref, small_ref, power_ref, sems = refs[7:]
    group = lax.axis_index("group")
    hidden_width, rank = panel_ref.shape
    width = w_ref.shape[0]
    done = FRONT * LANES if has_other else hidden_width
    if has_other:
        unpack_gram(rest_ref, other_full, 1)
        small_ref[:done, :] = panel_ref[:done, :].astype(BF16)
        small_ref[done:, :] = (
            panel_ref[done:, :] + product(other_full[done:, done:], first_ref[done:, :], NN)
        ).astype(BF16)
    else:
        small_ref[...] = panel_ref[...].astype(BF16)
    for first in range(0, hidden_width, LANES):
        rows = slice(first, first + LANES)
        if first < done:
            full_ref[rows, :] = own_ref[rows, :]
        else:
            full_ref[rows, :done] = own_ref[rows, :done] + front_ref[rows, :done].astype(F32)
            full_ref[rows, done:] = own_ref[rows, done:] + other_full[rows, done:].astype(F32)
        high_ref[rows, :] = full_ref[rows, :].astype(BF16)
    panel_rows = gram_out.shape[0]
    gram_copy = pltpu.make_async_copy(
        full_ref.at[pl.ds(pl.multiple_of(group * panel_rows, panel_rows), panel_rows), :],
        gram_out,
        sems.at[0],
    )
    gram_copy.start()
    panel = small_ref[...]
    reduced = product(square_ref[...], panel, NN)
    squares = jnp.sum(panel.astype(F32) * reduced, axis=0, keepdims=True)
    factor = lax.rsqrt(jnp.maximum(squares, 0.0) * (1.0 / width) + 1e-06)
    small_ref[...] = (reduced * factor).astype(BF16)
    small_ref[...] = product(high_ref[...], small_ref[...], NN).astype(BF16)
    own_rows = power_ref.shape[0]

    def power_copy(first, rows):
        part = pl.ds(first, rows)
        return pltpu.make_async_copy(
            power_ref.at[part, :], power_out.at[part, :], sems.at[1 + first // rows]
        )

    def power_step(first, rows, carry):
        mine = pl.ds(pl.multiple_of(group * own_rows + first, rows), rows)
        power_ref[pl.ds(first, rows), :] = product(w_ref[mine, :], small_ref[...], NN)
        power_copy(first, rows).start()
        return carry

    def power_wait(first, rows, carry):
        power_copy(first, rows).wait()
        return carry

    blocks_of(own_rows, 4 * LANES, power_step)
    gram_copy.wait()
    blocks_of(own_rows, 4 * LANES, power_wait)


def power(own, other, panel, reduced, w_down, square, group_count):
    width, hidden_width = w_down.shape
    rank = panel.shape[1]
    own_rows = width // group_count
    operands = [own, panel, *other]
    operands += [reduced[0], w_down, square]
    anywhere = pl.BlockSpec(memory_space=pl.ANY)
    return pl.pallas_call(
        functools.partial(power_kernel, has_other=len(other) > 0),
        out_shape=(
            jax.ShapeDtypeStruct((hidden_width // group_count, hidden_width), F32),
            jax.ShapeDtypeStruct((own_rows, rank), F32),
        ),
        in_specs=[VMEM] * len(operands),
        out_specs=(anywhere, anywhere),
        scratch_shapes=[
            pltpu.VMEM((hidden_width, hidden_width), F32),
            pltpu.VMEM((hidden_width, hidden_width), BF16),
            pltpu.VMEM((hidden_width, hidden_width), BF16),
            pltpu.VMEM((hidden_width, rank), BF16),
            pltpu.VMEM((own_rows, rank), F32),
            pltpu.SemaphoreType.DMA((1 + max(1, own_rows // (4 * LANES)),)),
        ],
        compiler_params=params(12),
        cost_estimate=pl.CostEstimate(
            flops=2 * rank * (6 * hidden_width * hidden_width + 3 * width * hidden_width),
            bytes_accessed=w_down.size * 4,
            transcendentals=0,
        ),
    )(*map(here, operands))


def ring_order(chips, across):
    depth = chips // across
    if across < 2 or depth % 2 or depth * across != chips:
        return list(range(chips))
    order = []
    for z in range(depth):
        row = range(1, across) if z % 2 == 0 else range(across - 1, 0, -1)
        order += [z * across + y for y in row]
    return order + [z * across for z in reversed(range(depth))]


def gram_of_all(halves, weights, tok_dev, scale, order, prepare):
    chips = len(order)
    onward = [
        (2 * order[i] + core, 2 * order[(i + 1) % chips] + core)
        for i in range(chips)
        for core in range(2)
    ]
    backward = [(b, a) for a, b in onward]
    sibling = [(i, i ^ 1) for i in range(2 * chips)]

    def send(array, pairs):
        return lax.ppermute(array, "expert", pairs)

    def swap(pieces):
        return [send(piece, sibling) for piece in pieces]

    slots = chips - 1
    sent = {1: (send(halves[0], onward), send(halves[1], backward))}
    weights_s = send(weights, sibling)
    *reduced, first, second = prepare(halves)
    sent[2] = (send(second, onward), send(first, backward))
    tie = reduced[0]
    groups = [(i, i + 1) for i in range(slots % 2, slots, 2)]
    groups = [(0,)] * (slots % 2) + groups
    work = {s: [] for s in range(1, slots + 1)}
    for group in groups:
        at = max(group[-1], 1)
        last = group == groups[-1]
        work[at].append((group, last))
        work[at if last or len(group) == 1 else at + 1].append((group, not last))
    blocks, mine, others, tiles = [halves], None, None, None
    for s in range(1, slots + 1):
        came = [after(tie, array) for array in sent[s]]
        if s + 2 <= slots:
            sent[s + 2] = (send(came[0], onward), send(came[1], backward))
        blocks.append(came if s % 2 else came[::-1])
        for group, for_sibling in work[s]:
            pieces = [half for i in group for half in blocks[i]]
            wait = [*came, tie]
            if for_sibling:
                gives = "tiles" if group == groups[-1] else "tie"
                others, tie = ffn(
                    weights_s, pieces, others, tok_dev, for_sibling=True, gives=gives, wait=wait
                )
                if gives == "tiles":
                    tiles = send(tie, sibling)
            else:
                mine, tie = ffn(weights, pieces, mine, tok_dev, wait=wait)
    swapped = swap(blocks[slots])
    tie = after(came[0], tie, came[1], hides=True)
    if tiles is not None:
        mine = merged(mine, tiles, tie)
    pieces = [*blocks[slots], *swapped]
    gram, front, hidden = ffn(weights, pieces, mine, tok_dev, gives="front", scale=scale, wait=[tie])
    gram, rest = rest_of(gram, hidden, scale)
    return gram, (front, rest), reduced


def on_device(tokens, routes, gate_up, down_weight, sketch):
    owner_count = lax.axis_size("expert")
    group_count = lax.axis_size("group")
    tok_dev = tokens.shape[1]
    order = ring_order(owner_count // 2, group_count)
    scale = 1.0 / (tok_dev * TOPK * group_count)
    halves = pack(tokens[0], routes[0].T)
    w_down = down_weight[0]
    own, packed, reduced = gram_of_all(
        halves,
        gate_up[0],
        tok_dev,
        scale,
        order,
        functools.partial(reduced_first, w_down, sketch[0]),
    )
    if group_count == 2:
        other = [lax.ppermute(part, "group", [(0, 1), (1, 0)]) for part in packed]
    else:
        own, other = lax.psum(own, "group"), []
    own, panel, w_down, square = own_side(own, *reduced, w_down)
    if other:
        own, panel, front = with_front(own, panel, other[0], reduced[0])
        other = [front, other[1]]
    gram, result = power(own, other, panel, reduced, w_down, square, group_count)
    return gram[None], result[None]


def solution(mesh):
    return jax.shard_map(
        on_device,
        mesh=mesh,
        in_specs=(
            P("group", "expert", None),
            P("group", "expert", None),
            P("expert", None, None),
            P("expert", None, None),
            P("expert", None, None),
        ),
        out_specs=(P("expert", "group", None), P("expert", "group", None)),
        check_vma=False,
    )
```

```python
import functools

import jax
import jax.numpy as jnp
from jax import lax
from jax.experimental import pallas as pl
from jax.experimental.pallas import tpu as pltpu
from jax.sharding import PartitionSpec as P

TOPK = 8
LANES = 128
FRONT = 2
ID_ROWS = 16
NT = (((1,), (1,)), ((), ()))
NN = (((1,), (0,)), ((), ()))
TN = (((0,), (0,)), ((), ()))
TT = (((0,), (1,)), ((), ()))
BF16 = jnp.bfloat16
F32 = jnp.float32
VMEM = pl.BlockSpec(memory_space=pltpu.VMEM)
MIB = 1 << 20


def here(array):
    return pltpu.with_memory_space_constraint(array, pltpu.VMEM)


def far(array):
    return pltpu.with_memory_space_constraint(array, pltpu.HBM)


def kept(shape, dtype):
    return pltpu.VMEM(tuple(shape), dtype)


def small_cost(hides):
    return pl.CostEstimate(flops=10**11 if hides else 1000, bytes_accessed=1000, transcendentals=0)


def params(mib):
    return pltpu.CompilerParams(vmem_limit_bytes=mib * MIB)


def half_rows(tok_dev, width):
    return tok_dev // 2 * (width // LANES) + ID_ROWS


def pack_kernel(tokens_hbm, routes_hbm, first_ref, second_ref, tokens_ref, routes_ref, sems):
    copies = [
        pltpu.make_async_copy(routes_hbm, routes_ref, sems.at[0]),
        pltpu.make_async_copy(tokens_hbm, tokens_ref, sems.at[1]),
    ]
    for copy in copies:
        copy.start()
    for copy in copies:
        copy.wait()
    tok_dev, width = tokens_ref.shape
    top = routes_ref.shape[0]
    half, tiles = tok_dev // 2, width // LANES
    rows = half_rows(tok_dev, width)
    ids = jnp.concatenate(
        [routes_ref[...].astype(F32), jnp.full((ID_ROWS - top, tok_dev), -1.0, F32)], axis=0
    )
    lane = lax.broadcasted_iota(jnp.int32, ids.shape, 1)
    for h, out_ref in enumerate((first_ref, second_ref)):
        for i in range(half // 16):
            for k in range(tiles):
                at = (i * tiles + k) * 16
                out_ref[at : at + 16, :] = tokens_ref[
                    h * half + i * 16 : h * half + (i + 1) * 16, k * LANES : (k + 1) * LANES
                ]
        mine = (lane >= h * half) & (lane < (h + 1) * half)
        out_ref[rows - ID_ROWS :, :tok_dev] = jnp.where(mine, ids, -1.0).astype(BF16)


def pack(tokens, routes):
    tok_dev, width = tokens.shape
    anywhere = pl.BlockSpec(memory_space=pl.ANY)
    return pl.pallas_call(
        pack_kernel,
        out_shape=(kept((half_rows(tok_dev, width), LANES), BF16),) * 2,
        in_specs=[anywhere, anywhere],
        out_specs=(VMEM, VMEM),
        scratch_shapes=[
            pltpu.VMEM(tokens.shape, tokens.dtype),
            pltpu.VMEM(routes.shape, routes.dtype),
            pltpu.SemaphoreType.DMA((2,)),
        ],
        compiler_params=params(2),
        cost_estimate=pl.CostEstimate(flops=0, bytes_accessed=tokens.size * 4, transcendentals=0),
    )(far(tokens), far(routes))


def split(value):
    high = value.astype(BF16)
    return high, (value - high.astype(F32)).astype(BF16)


def product(left, right, dims):
    return lax.dot_general(left, right, dims, preferred_element_type=F32)


def reduce_kernel(w_hbm, sketch_hbm, *refs):
    *halves, high_ref, low_ref = refs[:4]
    *again, w_ref, sketch_ref, sems = refs[4:]
    copies = [
        pltpu.make_async_copy(w_hbm, w_ref, sems.at[0]),
        pltpu.make_async_copy(sketch_hbm, sketch_ref, sems.at[1]),
    ]
    for copy in copies:
        copy.start()
    for copy in copies:
        copy.wait()
    high_ref[...], low_ref[...] = split(product(w_ref[...], sketch_ref[...], TN))
    for half, copied in zip(halves, again):
        copied[...] = half[...]


def reduced_first(w_down, sketch, halves):
    half = kept((w_down.shape[1], sketch.shape[1]), BF16)
    anywhere = pl.BlockSpec(memory_space=pl.ANY)
    return pl.pallas_call(
        reduce_kernel,
        out_shape=(half, half, *(kept(array.shape, array.dtype) for array in halves)),
        in_specs=[anywhere, anywhere, VMEM, VMEM],
        out_specs=(VMEM,) * 4,
        scratch_shapes=[
            pltpu.VMEM(w_down.shape, w_down.dtype),
            pltpu.VMEM(sketch.shape, sketch.dtype),
            pltpu.SemaphoreType.DMA((2,)),
        ],
        compiler_params=params(6),
        cost_estimate=small_cost(True),
    )(far(w_down), far(sketch), *map(here, halves))


def nothing_kernel(*refs):
    pass


def after(tie, array, *others, hides=False):
    operands = (array, tie, *others)
    return pl.pallas_call(
        nothing_kernel,
        out_shape=kept(array.shape, array.dtype),
        in_specs=[VMEM] * len(operands),
        out_specs=VMEM,
        input_output_aliases={0: 0},
        compiler_params=params(2),
        cost_estimate=small_cost(hides),
    )(*map(here, operands))


def right_tiles(count, part):
    rows = range(count)[:FRONT] if part == 0 else range(count)[FRONT:]
    return [(a, b) for a in rows for b in range(a + 1, count)]


def pairs_of(count, part):
    return range(0, min(count, FRONT), 2) if part == 0 else range(FRONT, count, 2)


def packed_rows(count, part):
    return (len(right_tiles(count, part)) + len(pairs_of(count, part))) * LANES + ID_ROWS


def tile_places():
    return (
        lax.broadcasted_iota(jnp.int32, (LANES, LANES), 0),
        lax.broadcasted_iota(jnp.int32, (LANES, LANES), 1),
    )


def gram_step(hidden_width):
    return 2 * LANES if hidden_width % (2 * LANES) == 0 else LANES


def pack_gram(gram_ref, packed_ref, part):
    count = gram_ref.shape[0] // LANES
    rights = right_tiles(count, part)

    def tile(a, b):
        return gram_ref[a * LANES : (a + 1) * LANES, b * LANES : (b + 1) * LANES]

    for at, (a, b) in enumerate(rights):
        packed_ref[at * LANES : (at + 1) * LANES, :] = tile(a, b).astype(BF16)
    row, column = tile_places()
    strip = jnp.zeros((ID_ROWS, LANES), F32)
    place = lax.broadcasted_iota(jnp.int32, strip.shape, 0)
    at = len(rights) * LANES
    for i, first in enumerate(pairs_of(count, part)):
        both = tile(first, first)
        if first + 1 < count:
            second = tile(first + 1, first + 1)
            diagonal = jnp.sum(jnp.where(row == column, second, 0.0), axis=0, keepdims=True)
            strip = jnp.where(place == i, diagonal, strip)
            both = jnp.where(row <= column, both, second)
        packed_ref[at : at + LANES, :] = both.astype(BF16)
        at += LANES
    packed_ref[at : at + ID_ROWS, :] = strip.astype(BF16)


def upper_tiles(count):
    return [(a, b) for a in range(count) for b in range(a, count)]


def tiles_of(gram_ref):
    for at, (a, b) in enumerate(upper_tiles(gram_ref.shape[0] // LANES)):
        yield (
            slice(at * LANES, (at + 1) * LANES),
            slice(a * LANES, (a + 1) * LANES),
            slice(b * LANES, (b + 1) * LANES),
        )


def unpack_gram(packed_ref, full_ref, part):
    count = full_ref.shape[0] // LANES
    rights = right_tiles(count, part)

    def put(a, b, value):
        full_ref[a * LANES : (a + 1) * LANES, b * LANES : (b + 1) * LANES] = value.astype(BF16)

    for at, (a, b) in enumerate(rights):
        value = packed_ref[at * LANES : (at + 1) * LANES, :]
        put(a, b, value)
        put(b, a, value.astype(F32).T)
    row, column = tile_places()
    pairs = pairs_of(count, part)
    at = (len(rights) + len(pairs)) * LANES
    strip = packed_ref[at : at + ID_ROWS, :].astype(F32)
    for i, first in enumerate(pairs):
        at = (len(rights) + i) * LANES
        both = packed_ref[at : at + LANES, :].astype(F32)
        turned = both.T
        put(first, first, jnp.where(row <= column, both, turned))
        if first + 1 < count:
            second = jnp.where(row > column, both, turned)
            second = jnp.where(row == column, strip[i : i + 1, :], second)
            put(first + 1, first + 1, second)


def ffn_kernel(*refs, tok_dev, width, operands, has_gram, for_sibling, gives, scale):
    weight_ref, pieces = refs[0], refs[1 : 1 + operands]
    rest = list(refs[1 + operands :])
    gram_in = rest.pop(0) if has_gram else None
    gram_out, last_out, hidden_ref, x_ref, mask_ref = rest[-5:]
    half, tiles = tok_dev // 2, width // LANES
    expert = lax.axis_index("expert")
    if for_sibling:
        expert = expert + 1 - 2 * (expert % 2)
    expert = expert.astype(F32)
    for b in range(operands // 2):
        hits = None
        for h in range(2):
            piece = pieces[2 * b + h]
            for i in range(half // 16):
                for k in range(tiles):
                    at = (i * tiles + k) * 16
                    row = b * tok_dev + h * half + i * 16
                    x_ref[row : row + 16, k * LANES : (k + 1) * LANES] = piece[at : at + 16, :]
            at = half * tiles
            found = (piece[at : at + ID_ROWS, :tok_dev].astype(F32) == expert).astype(F32)
            hits = found if hits is None else hits + found
        mask_ref[0:1, b * tok_dev : (b + 1) * tok_dev] = jnp.max(hits, axis=0, keepdims=True)
    hidden_width = weight_ref.shape[1] // 2
    step_rows = gram_step(hidden_width)

    gate = product(weight_ref[:, :hidden_width], x_ref[...], TT)
    up = product(weight_ref[:, hidden_width:], x_ref[...], TT)
    hidden_ref[...] = (gate * (0.5 * jnp.tanh(0.5 * gate) + 0.5) * up * mask_ref[0:1, :]).astype(BF16)
    for first in range(0, FRONT * LANES if gives == "front" else hidden_width, step_rows):
        gram_rows(hidden_ref, gram_in, gram_out, first, step_rows, scale)
    if gives == "front":
        pack_gram(gram_out, last_out, 0)
    elif gives == "tiles":
        for at, rows, columns in tiles_of(gram_out):
            last_out[at, :] = gram_out[rows, columns].astype(BF16)
    else:
        last_out[...] = jnp.zeros_like(last_out)


def gram_rows(hidden_ref, gram_in, gram_out, first, count, scale):
    rows = slice(first, first + count)
    part = product(hidden_ref[rows, :], hidden_ref[first:, :], NT)
    if gram_in is not None:
        part += gram_in[rows, first:]
    gram_out[rows, first:] = part * scale


def rest_kernel(gram_in, hidden_ref, gram_out, packed_out, *, scale):
    hidden_width = gram_in.shape[0]
    step_rows = gram_step(hidden_width)
    for first in range(FRONT * LANES, hidden_width, step_rows):
        gram_rows(hidden_ref, gram_in, gram_out, first, step_rows, scale)
    pack_gram(gram_out, packed_out, 1)


def rest_of(gram, hidden, scale):
    count = gram.shape[0] // LANES
    return pl.pallas_call(
        functools.partial(rest_kernel, scale=scale),
        out_shape=(kept(gram.shape, gram.dtype), kept((packed_rows(count, 1), LANES), BF16)),
        in_specs=[VMEM, VMEM],
        out_specs=(VMEM, VMEM),
        input_output_aliases={0: 0},
        compiler_params=params(10),
        cost_estimate=small_cost(False),
    )(here(gram), here(hidden))


def ffn(
    weights,
    pieces,
    gram,
    tok_dev,
    for_sibling=False,
    gives="tie",
    scale=1.0,
    wait=(),
):
    hidden_width, width = weights.shape[1] // 2, weights.shape[0]
    count = hidden_width // LANES
    rows = tok_dev * len(pieces) // 2
    last = {
        "tie": kept((8, LANES), F32),
        "tiles": kept((len(upper_tiles(count)) * LANES, LANES), BF16),
        "front": kept((packed_rows(count, 0), LANES), BF16),
    }[gives]
    hidden = pltpu.VMEM((hidden_width, rows), BF16)
    front = gives == "front"
    operands = [weights, *pieces, *([] if gram is None else [gram]), *wait]
    return pl.pallas_call(
        functools.partial(
            ffn_kernel,
            tok_dev=tok_dev,
            width=width,
            operands=len(pieces),
            has_gram=gram is not None,
            for_sibling=for_sibling,
            gives=gives,
            scale=scale,
        ),
        out_shape=(kept((hidden_width, hidden_width), F32), last, *([hidden] * front)),
        in_specs=[VMEM] * len(operands),
        out_specs=(VMEM,) * (2 + front),
        input_output_aliases={} if gram is None else {1 + len(pieces): 0},
        scratch_shapes=[
            *([hidden] * (not front)),
            pltpu.VMEM((rows, width), BF16),
            pltpu.VMEM((8, rows), F32),
        ],
        compiler_params=params(8),
        cost_estimate=small_cost(False),
    )(*map(here, operands))


def merge_kernel(gram_ref, tiles_ref, tie_ref, out_ref):
    for at, rows, columns in tiles_of(gram_ref):
        out_ref[rows, columns] = gram_ref[rows, columns] + tiles_ref[at, :].astype(F32)


def merged(gram, tiles, tie):
    return pl.pallas_call(
        merge_kernel,
        out_shape=kept(gram.shape, gram.dtype),
        in_specs=[VMEM] * 3,
        out_specs=VMEM,
        input_output_aliases={0: 0},
        compiler_params=params(10),
        cost_estimate=small_cost(False),
    )(here(gram), here(tiles), here(tie))


def exact(high, low, other_high, other_low):
    total = product(low, other_high, NN)
    total += product(high, other_low, NN)
    return total + product(high, other_high, NN)


def own_kernel(own_ref, high_ref, low_ref, w_hbm, full_ref, panel_ref, w_ref, square_ref, sem):
    copy = pltpu.make_async_copy(w_hbm, w_ref, sem)
    copy.start()
    for _, rows, columns in tiles_of(own_ref):
        tile = own_ref[rows, columns]
        full_ref[rows, columns] = tile
        if rows != columns:
            full_ref[columns, rows] = tile.T
    hidden_width = own_ref.shape[0]
    step_rows = gram_step(hidden_width)
    for first in range(0, hidden_width, step_rows):
        rows = slice(first, first + step_rows)
        high, low = split(full_ref[rows, :])
        panel_ref[rows, :] = exact(high, low, high_ref[...], low_ref[...])
    copy.wait()
    for first in range(0, hidden_width, step_rows):
        rows = slice(first, first + step_rows)
        square_ref[rows, :] = product(w_ref[:, rows], w_ref[...], TN).astype(BF16)


def own_side(own, high, low, w_down):
    hidden_width, rank = high.shape
    return pl.pallas_call(
        own_kernel,
        out_shape=(
            kept((hidden_width, hidden_width), F32),
            kept((hidden_width, rank), F32),
            kept(w_down.shape, w_down.dtype),
            kept((hidden_width, hidden_width), BF16),
        ),
        in_specs=[VMEM] * 3 + [pl.BlockSpec(memory_space=pl.ANY)],
        out_specs=(VMEM,) * 4,
        scratch_shapes=[pltpu.SemaphoreType.DMA],
        compiler_params=params(6),
        cost_estimate=small_cost(False),
    )(here(own), here(high), here(low), far(w_down))


def blocks_of(total, most, step, carry=None):
    rows = most if total % most == 0 else total
    return lax.fori_loop(
        0, total // rows, lambda i, c: step(pl.multiple_of(i * rows, rows), rows, c), carry
    )


def front_kernel(own_in, panel_in, front_ref, first_ref, own_out, panel_out, other_ref):
    rows = slice(0, FRONT * LANES)
    other_ref[FRONT * LANES :, FRONT * LANES :] = jnp.zeros_like(
        other_ref[FRONT * LANES :, FRONT * LANES :]
    )
    unpack_gram(front_ref, other_ref, 0)
    panel_out[...] = panel_in[...] + product(other_ref[...], first_ref[...], NN)
    own_out[rows, :] = own_in[rows, :] + other_ref[rows, :].astype(F32)


def with_front(own, panel, front, first):
    return pl.pallas_call(
        front_kernel,
        out_shape=(
            kept(own.shape, F32),
            kept(panel.shape, F32),
            kept(own.shape, BF16),
        ),
        in_specs=[VMEM] * 4,
        out_specs=(VMEM,) * 3,
        input_output_aliases={0: 0, 1: 1},
        compiler_params=params(10),
        cost_estimate=small_cost(False),
    )(*map(here, (own, panel, front, first)))


def power_kernel(*refs, has_other):
    refs = list(refs)
    own_ref, panel_ref = refs[:2]
    front_ref, rest_ref = [refs.pop(2) for _ in range(2)] if has_other else (None, None)
    first_ref, w_ref, square_ref, gram_out, power_out = refs[2:7]
    full_ref, other_full, high_ref, small_ref, power_ref, sems = refs[7:]
    group = lax.axis_index("group")
    hidden_width, rank = panel_ref.shape
    width = w_ref.shape[0]
    done = FRONT * LANES if has_other else hidden_width
    if has_other:
        unpack_gram(rest_ref, other_full, 1)
        small_ref[:done, :] = panel_ref[:done, :].astype(BF16)
        small_ref[done:, :] = (
            panel_ref[done:, :] + product(other_full[done:, done:], first_ref[done:, :], NN)
        ).astype(BF16)
    else:
        small_ref[...] = panel_ref[...].astype(BF16)
    for first in range(0, hidden_width, LANES):
        rows = slice(first, first + LANES)
        if first < done:
            full_ref[rows, :] = own_ref[rows, :]
        else:
            full_ref[rows, :done] = own_ref[rows, :done] + front_ref[rows, :done].astype(F32)
            full_ref[rows, done:] = own_ref[rows, done:] + other_full[rows, done:].astype(F32)
        high_ref[rows, :] = full_ref[rows, :].astype(BF16)
    panel_rows = gram_out.shape[0]
    gram_copy = pltpu.make_async_copy(
        full_ref.at[pl.ds(pl.multiple_of(group * panel_rows, panel_rows), panel_rows), :],
        gram_out,
        sems.at[0],
    )
    gram_copy.start()
    panel = small_ref[...]
    reduced = product(square_ref[...], panel, NN)
    squares = jnp.sum(panel.astype(F32) * reduced, axis=0, keepdims=True)
    factor = lax.rsqrt(jnp.maximum(squares, 0.0) * (1.0 / width) + 1e-06)
    small_ref[...] = (reduced * factor).astype(BF16)
    small_ref[...] = product(high_ref[...], small_ref[...], NN).astype(BF16)
    own_rows = power_ref.shape[0]

    def power_copy(first, rows):
        part = pl.ds(first, rows)
        return pltpu.make_async_copy(
            power_ref.at[part, :], power_out.at[part, :], sems.at[1 + first // rows]
        )

    def power_step(first, rows, carry):
        mine = pl.ds(pl.multiple_of(group * own_rows + first, rows), rows)
        power_ref[pl.ds(first, rows), :] = product(w_ref[mine, :], small_ref[...], NN)
        for at in range(0, rows, LANES):
            power_copy(first + at, LANES).start()
        return carry

    def power_wait(first, rows, carry):
        power_copy(first, rows).wait()
        return carry

    blocks_of(own_rows, 4 * LANES, power_step)
    gram_copy.wait()
    blocks_of(own_rows, LANES, power_wait)


def power(own, other, panel, reduced, w_down, square, group_count):
    width, hidden_width = w_down.shape
    rank = panel.shape[1]
    own_rows = width // group_count
    operands = [own, panel, *other]
    operands += [reduced[0], w_down, square]
    anywhere = pl.BlockSpec(memory_space=pl.ANY)
    return pl.pallas_call(
        functools.partial(power_kernel, has_other=len(other) > 0),
        out_shape=(
            jax.ShapeDtypeStruct((hidden_width // group_count, hidden_width), F32),
            jax.ShapeDtypeStruct((own_rows, rank), F32),
        ),
        in_specs=[VMEM] * len(operands),
        out_specs=(anywhere, anywhere),
        scratch_shapes=[
            pltpu.VMEM((hidden_width, hidden_width), F32),
            pltpu.VMEM((hidden_width, hidden_width), BF16),
            pltpu.VMEM((hidden_width, hidden_width), BF16),
            pltpu.VMEM((hidden_width, rank), BF16),
            pltpu.VMEM((own_rows, rank), F32),
            pltpu.SemaphoreType.DMA((1 + own_rows // LANES,)),
        ],
        compiler_params=params(12),
        cost_estimate=pl.CostEstimate(
            flops=2 * rank * (6 * hidden_width * hidden_width + 3 * width * hidden_width),
            bytes_accessed=w_down.size * 4,
            transcendentals=0,
        ),
    )(*map(here, operands))


def ring_order(chips, across):
    depth = chips // across
    if across < 2 or depth % 2 or depth * across != chips:
        return list(range(chips))
    order = []
    for z in range(depth):
        row = range(1, across) if z % 2 == 0 else range(across - 1, 0, -1)
        order += [z * across + y for y in row]
    return order + [z * across for z in reversed(range(depth))]


def gram_of_all(halves, weights, tok_dev, scale, order, prepare):
    chips = len(order)
    onward = [
        (2 * order[i] + core, 2 * order[(i + 1) % chips] + core)
        for i in range(chips)
        for core in range(2)
    ]
    backward = [(b, a) for a, b in onward]
    sibling = [(i, i ^ 1) for i in range(2 * chips)]

    def send(array, pairs):
        return lax.ppermute(array, "expert", pairs)

    def swap(pieces):
        return [send(piece, sibling) for piece in pieces]

    slots = chips - 1
    sent = {1: (send(halves[0], onward), send(halves[1], backward))}
    weights_s = send(weights, sibling)
    *reduced, first, second = prepare(halves)
    sent[2] = (send(second, onward), send(first, backward))
    tie = reduced[0]
    groups = [(i, i + 1) for i in range(slots % 2, slots, 2)]
    groups = [(0,)] * (slots % 2) + groups
    work = {s: [] for s in range(1, slots + 1)}
    for group in groups:
        at = max(group[-1], 1)
        last = group == groups[-1]
        work[at].append((group, last))
        work[at if last or len(group) == 1 else at + 1].append((group, not last))
    blocks, mine, others, tiles = [halves], None, None, None
    for s in range(1, slots + 1):
        came = [after(tie, array) for array in sent[s]]
        if s + 2 <= slots:
            sent[s + 2] = (send(came[0], onward), send(came[1], backward))
        blocks.append(came if s % 2 else came[::-1])
        for group, for_sibling in work[s]:
            pieces = [half for i in group for half in blocks[i]]
            wait = [*came, tie]
            if for_sibling:
                gives = "tiles" if group == groups[-1] else "tie"
                others, tie = ffn(
                    weights_s, pieces, others, tok_dev, for_sibling=True, gives=gives, wait=wait
                )
                if gives == "tiles":
                    tiles = send(tie, sibling)
            else:
                mine, tie = ffn(weights, pieces, mine, tok_dev, wait=wait)
    swapped = swap(blocks[slots])
    tie = after(came[0], tie, came[1], hides=True)
    if tiles is not None:
        mine = merged(mine, tiles, tie)
    pieces = [*blocks[slots], *swapped]
    gram, front, hidden = ffn(weights, pieces, mine, tok_dev, gives="front", scale=scale, wait=[tie])
    gram, rest = rest_of(gram, hidden, scale)
    return gram, (front, rest), reduced


def on_device(tokens, routes, gate_up, down_weight, sketch):
    owner_count = lax.axis_size("expert")
    group_count = lax.axis_size("group")
    tok_dev = tokens.shape[1]
    order = ring_order(owner_count // 2, group_count)
    scale = 1.0 / (tok_dev * TOPK * group_count)
    halves = pack(tokens[0], routes[0].T)
    w_down = down_weight[0]
    own, packed, reduced = gram_of_all(
        halves,
        gate_up[0],
        tok_dev,
        scale,
        order,
        functools.partial(reduced_first, w_down, sketch[0]),
    )
    if group_count == 2:
        other = [lax.ppermute(part, "group", [(0, 1), (1, 0)]) for part in packed]
    else:
        own, other = lax.psum(own, "group"), []
    own, panel, w_down, square = own_side(own, *reduced, w_down)
    if other:
        own, panel, front = with_front(own, panel, other[0], reduced[0])
        other = [front, other[1]]
    gram, result = power(own, other, panel, reduced, w_down, square, group_count)
    return gram[None], result[None]


def solution(mesh):
    return jax.shard_map(
        on_device,
        mesh=mesh,
        in_specs=(
            P("group", "expert", None),
            P("group", "expert", None),
            P("expert", None, None),
            P("expert", None, None),
            P("expert", None, None),
        ),
        out_specs=(P("expert", "group", None), P("expert", "group", None)),
        check_vma=False,
    )
```
